32 devices in a mesh: tm: 2 (over core), cell: 16 (over z, y, x).
Axes of the slice: x: 2, y: 2, z: 4, core: 2. Of those that a mesh axis runs over, the one named last changes fastest.
Arguments:
- block_rows: int32 [2, 1024], P('tm', 'cell'), may hold values from 0 to 63, as said below
- block_cols: int32 [2, 1024], P('tm', 'cell'), may hold values from 0 to 63, as said below
- block_values: bfloat16 [2, 1024, 128, 128], P('tm', 'cell'), as said below
- growth: float32 [2, 8192], P('tm', 'cell'), may hold values from 0.5 to 4
- first_labels: int32 [8, 8192], P(None, 'cell'), may hold values from 0 to 15, as said below
- last_labels: int32 [8, 8192], P(None, 'cell'), may hold values from 0 to 15
Outputs:
- forward_mass: bfloat16 [2, 128, 8192], P('tm', None, 'cell')
- fate: bfloat16 [2, 128, 8192], P('tm', None, 'cell')
The draws below stay inside these ranges and needn't reach their ends.
Inputs may be any that keep to these rules, and one draw needn't show every extreme that they name: `block_rows`: the slots n of a coupling with n // 64 = c name row blocks c * 4 to (c + 1) * 4 - 1 only, and each row block is named by exactly 16 slots of each coupling. `block_cols`: A slot's column block differs from its row block by at most 4; a pair of row and column block may stand in several slots, whose blocks then add. `block_values`: every entry is positive. `first_labels`: in every panel each of the 16 types labels exactly 512 cells.
All inputs are finite; a program needn't handle non-finite values.
Results may differ from the reference program's by a relative error of at most 0.006.
Values may be sent and summed in bfloat16 or wider, within the bound.
No kernel may reach another device: no remote copies, remote signals or barrier semaphores. Data moves between devices by JAX's collectives and lax.ppermute only.
A program may use at most 64 MiB of HBM per device.

```python
import math
import jax
import jax.numpy as jnp
from jax import lax

CELL_TYPES = 16
BLOCK_SIDE = 128
PER_ROW = 16
BAND_REACH = 4
DEV_BLOCKS = 4
PANELS = 8
ALL_CELLS = 8192
TIME_BLOCKS = 64
DEV_SLOTS = 64
ALL_SLOTS = 1024
COUPLINGS = 2
COLUMNS = 128
N_CELL = 16


def band_pairs(key):
    rows_key = jax.random.fold_in(key, 11)
    offset_key = jax.random.fold_in(key, 12)
    keys = jax.random.split(rows_key, COUPLINGS * N_CELL)

    def one_order(one_key):
        return jax.random.permutation(one_key, DEV_SLOTS)
    orders = jax.vmap(one_order)(keys).reshape(COUPLINGS, N_CELL, DEV_SLOTS)
    owner = jnp.arange(N_CELL, dtype=jnp.int32)[None, :, None]
    row_ids = (owner * DEV_BLOCKS + orders // PER_ROW).reshape(COUPLINGS, ALL_SLOTS).astype(jnp.int32)
    offsets = jax.random.randint(offset_key, (COUPLINGS, ALL_SLOTS), -BAND_REACH, BAND_REACH + 1)
    col_ids = row_ids + offsets
    col_ids = jnp.where(col_ids < 0, -col_ids, col_ids)
    col_ids = jnp.where(col_ids > TIME_BLOCKS - 1, 2 * (TIME_BLOCKS - 1) - col_ids, col_ids)
    return (row_ids, col_ids.astype(jnp.int32))


def draw_block_rows(key, part):
    row_ids, col_ids = band_pairs(key)
    return row_ids


def draw_block_cols(key, part):
    row_ids, col_ids = band_pairs(key)
    return col_ids


def draw_block_values(key, part):
    row_ids, col_ids = band_pairs(key)
    value_key = jax.random.fold_in(key, 21)
    col_key = jax.random.fold_in(key, 23)
    full_shape = (COUPLINGS, ALL_SLOTS, BLOCK_SIDE, BLOCK_SIDE)
    rise = 1.0 + 2.0 * col_ids.astype(jnp.float32) / (TIME_BLOCKS - 1)
    col_scale = jnp.exp(jax.random.uniform(col_key, (COUPLINGS, ALL_SLOTS, 1, BLOCK_SIDE), jnp.float32, 0.0, math.log(10.0)))
    entries = jnp.exp(jax.random.uniform(value_key, full_shape, jnp.float32, math.log(0.05), 0.0))
    scaled = entries * col_scale * rise[:, :, None, None] / (PER_ROW * BLOCK_SIDE)
    return scaled.astype(jnp.bfloat16)


def draw_first_labels(key, part):
    keys = jax.random.split(jax.random.fold_in(key, 31), PANELS)

    def one_panel(one_key):
        return jax.random.permutation(one_key, ALL_CELLS) % CELL_TYPES
    return jax.vmap(one_panel)(keys).astype(jnp.int32)


def place_ends(array, stream_key, smallest, high):
    spot = [jax.random.randint(jax.random.fold_in(stream_key, axis), (), 0, length) for axis, length in enumerate(array.shape)]
    longest = array.shape.index(max(array.shape))
    next_to = spot[:longest] + [(spot[longest] + 1) % array.shape[longest]] + spot[longest + 1:]
    return array.at[tuple(spot)].set(smallest).at[tuple(next_to)].set(high)


def steps_of(key, extent, shards, low, high):
    loudness, own = 1.0, jax.random.fold_in(key, 6)
    for position, parts in shards:
        draws = jnp.exp(jax.random.uniform(jax.random.fold_in(own, position), (parts,), jnp.float32, low / len(shards), high / len(shards)))
        loudness = loudness * jnp.repeat(draws, extent[position] // parts).reshape([-1 if axis == position else 1 for axis in range(len(extent))])
    return loudness


def setup_inputs(seed: int = 0) -> dict:
    key_list = jax.random.split(jax.random.key(seed), 7)
    return {
        "block_rows": draw_block_rows(jax.random.fold_in(key_list[6], 71), 0),
        "block_cols": draw_block_cols(jax.random.fold_in(key_list[6], 71), 0),
        "block_values": draw_block_values(jax.random.fold_in(key_list[6], 71), 0),
        "growth": jnp.clip(jnp.exp(math.log(4.0) - 2.0794415 * jax.random.uniform(key_list[3], (COUPLINGS, ALL_CELLS), jnp.float32) ** steps_of(key_list[3], (COUPLINGS, ALL_CELLS), ((0, 2), (1, 16)), -0.2, 0.2)), 0.5, 4.0),
        "first_labels": draw_first_labels(jax.random.fold_in(key_list[6], 71), 0),
        "last_labels": place_ends(jax.random.randint(key_list[5], (PANELS, ALL_CELLS), 0, CELL_TYPES), jax.random.fold_in(key_list[5], 1), 0, CELL_TYPES - 1).astype(jnp.int32),
    }


def seed_stack(labels):
    marks = labels[:, None, :] == jnp.arange(CELL_TYPES, dtype=jnp.int32)[None, :, None]
    return marks.astype(jnp.bfloat16).reshape(COLUMNS, ALL_CELLS)


def forward_step(stack_in, row_ids, col_ids, blocks, growth_row):
    scaled = (stack_in.astype(jnp.float32) / growth_row[None, :]).astype(jnp.bfloat16)
    picked = scaled.reshape(COLUMNS, TIME_BLOCKS, BLOCK_SIDE)[:, row_ids, :]
    carried = jnp.einsum("qsk,skl->qsl", picked.astype(jnp.float32), blocks.astype(jnp.float32))
    summed = jnp.zeros((COLUMNS, TIME_BLOCKS, BLOCK_SIDE), jnp.float32).at[:, col_ids, :].add(carried)
    totals = jnp.sum(summed, axis=(1, 2))
    return (summed * (ALL_CELLS / totals)[:, None, None]).astype(jnp.bfloat16).reshape(COLUMNS, ALL_CELLS)


def backward_step(stack_in, row_ids, col_ids, blocks):
    picked = stack_in.reshape(COLUMNS, TIME_BLOCKS, BLOCK_SIDE)[:, col_ids, :]
    pulled = jnp.einsum("skl,qsl->qsk", blocks.astype(jnp.float32), picked.astype(jnp.float32))
    summed = jnp.zeros((COLUMNS, TIME_BLOCKS, BLOCK_SIDE), jnp.float32).at[:, row_ids, :].add(pulled)
    grouped = summed.reshape(PANELS, CELL_TYPES, TIME_BLOCKS, BLOCK_SIDE)
    fates = grouped * (CELL_TYPES / jnp.sum(grouped, axis=1, keepdims=True))
    return fates.astype(jnp.bfloat16).reshape(COLUMNS, ALL_CELLS)


def reference(block_rows, block_cols, block_values, growth, first_labels, last_labels):
    def forward_turn(stack_in, inputs):
        result = forward_step(stack_in, inputs[0], inputs[1], inputs[2], inputs[3])
        return result, result

    final_mass, forward_mass = lax.scan(forward_turn, seed_stack(first_labels), (block_rows, block_cols, block_values, growth))

    def backward_turn(stack_in, inputs):
        result = backward_step(stack_in, inputs[0], inputs[1], inputs[2])
        return result, result

    first_fate, fate = lax.scan(backward_turn, seed_stack(last_labels), (block_rows, block_cols, block_values), reverse=True)
    return forward_mass, fate
```

```python
import functools
import jax
import jax.numpy as jnp
from jax import lax
from jax.experimental import pallas as pl
from jax.experimental.pallas import tpu as pltpu
from jax.sharding import PartitionSpec as P

CELL_TYPES = 16
BAND_REACH = 4
LABEL_ROWS = 16
CHUNKS = 8


def rows_of(block, side):
    return pl.ds(pl.multiple_of(block * side, side), side)


def as_column(row, side):
    return jnp.transpose(jnp.broadcast_to(row, (side, side)))


def as_row(column, side):
    return jnp.transpose(jnp.broadcast_to(column, (side, side)))[0:8]


def one_hot(labels):
    types = lax.broadcasted_iota(jnp.int32, (CELL_TYPES, labels.shape[1]), 0)
    return jnp.concatenate([labels[p : p + 1] == types for p in range(labels.shape[0])], axis=0)


def load_blocks(blocks_hbm, blk, sems):
    part = blk.shape[0] // CHUNKS
    return [
        pltpu.make_async_copy(blocks_hbm.at[0, pl.ds(i * part, part)], blk.at[pl.ds(i * part, part)], sems.at[i])
        for i in range(CHUNKS)
    ]


def push_forward(rows_ref, cols_ref, src, blk, acc, first_row, first_col, copies):
    side = blk.shape[1]
    acc[...] = jnp.zeros_like(acc)
    part = blk.shape[0] // CHUNKS
    for n in range(blk.shape[0]):
        if copies is not None and n % part == 0:
            copies[n // part].wait()
        row = rows_of(rows_ref[0, n] - first_row, side)
        col = rows_of(cols_ref[0, n] - first_col, side)
        acc[col, :] += jnp.dot(src[row, :], blk[n], preferred_element_type=jnp.float32)


def pull_backward(rows_ref, cols_ref, src, blk, acc, first_row, first_col, copies):
    side = blk.shape[1]
    acc[...] = jnp.zeros_like(acc)
    part = blk.shape[0] // CHUNKS
    for n in range(blk.shape[0]):
        if copies is not None and n % part == 0:
            copies[n // part].wait()
        row = rows_of(rows_ref[0, n] - first_row, side)
        col = rows_of(cols_ref[0, n] - first_col, side)
        acc[row, :] += lax.dot_general(
            src[col, :], blk[n], (((1,), (1,)), ((), ())), preferred_element_type=jnp.float32
        )


def fates_of(pulled):
    height, cells = pulled.shape
    grouped = pulled.reshape(height // CELL_TYPES, CELL_TYPES, cells)
    scale = CELL_TYPES / jnp.sum(grouped, axis=1, keepdims=True)
    return (grouped * scale).reshape(height, cells).astype(jnp.bfloat16)


def first_kernel(own, rows_ref, cols_ref, growth_ref, first_ref, last_ref, blocks_hbm,
                 left_ref, mid_ref, right_ref, keep_ref, part_ref, half_ref, blk, src, acc, sems):
    side = blk.shape[1]
    first_row = lax.axis_index("cell") * own
    copies = load_blocks(blocks_hbm, blk, sems)
    for copy in copies:
        copy.start()

    @pl.when(lax.axis_index("tm") == 0)
    def _():
        for b in range(own):
            cells = pl.ds(b * side, side)
            inverse = 1.0 / growth_ref[0:1, cells]
            hot = one_hot(first_ref[:, cells])
            src[pl.ds(b * side, side), :] = jnp.where(hot, inverse, 0.0).astype(jnp.bfloat16)
        push_forward(rows_ref, cols_ref, src, blk, acc, first_row, first_row - BAND_REACH, copies)
        reach = BAND_REACH * side
        inner = own * side
        left_ref[0:reach, :] = acc[0:reach, :].astype(jnp.bfloat16)
        mid_ref[...] = acc[reach : reach + inner, :].astype(jnp.bfloat16)
        right_ref[0:reach, :] = acc[reach + inner :, :].astype(jnp.bfloat16)
        keep_ref[...] = acc[reach : reach + inner, :]
        for b in range(own):
            labels = last_ref[:, b * side : (b + 1) * side].astype(jnp.float32).astype(jnp.bfloat16)
            tall = jnp.concatenate([labels, labels], axis=0)
            left_ref[pl.ds(reach + b * LABEL_ROWS, LABEL_ROWS), :] = tall
            right_ref[pl.ds(reach + b * LABEL_ROWS, LABEL_ROWS), :] = tall
        total = acc[0:side, :]
        for w in range(1, own + 2 * BAND_REACH):
            total += acc[w * side : (w + 1) * side, :]
        sums = jnp.sum(jnp.transpose(total), axis=0, keepdims=True)
        part_ref[0:8, :] = jnp.broadcast_to(sums, (8, side))
        part_ref[8:16, :] = jnp.zeros((8, side), jnp.float32)
        half_ref[...] = jnp.zeros_like(half_ref)

    @pl.when(lax.axis_index("tm") != 0)
    def _():
        for copy in copies:
            copy.wait()
        largest = blk[0].astype(jnp.float32)
        for n in range(1, blk.shape[0]):
            largest = jnp.maximum(largest, blk[n].astype(jnp.float32))
        top = jnp.max(jnp.max(largest, axis=0, keepdims=True), axis=1, keepdims=True)
        half = jnp.round(0.5 * jnp.log2(jnp.maximum(top, 2.0**-126)))
        half_ref[...] = jnp.broadcast_to(half, half_ref.shape)


def second_kernel(own, rows_ref, cols_ref, growth_ref, last_ref, left_ref, mid_ref, right_ref, part_in, half_ref,
                  blocks_hbm, to_left, to_mid, to_right, keep_ref, part_ref, blk, src, acc, fated, pulled, sems):
    side = blk.shape[1]
    here = lax.axis_index("cell")
    first_row = here * own
    reach, inner = BAND_REACH * side, own * side

    @pl.when(lax.axis_index("tm") == 0)
    def _():
        part_ref[...] = part_in[...]

    @pl.when(lax.axis_index("tm") != 0)
    def _():
        copies = load_blocks(blocks_hbm, blk, sems)
        for copy in copies:
            copy.start()
        has_left, has_right = here > 0, here < lax.axis_size("cell") - 1
        sides = []
        mass = []
        for b in range(own):
            at = pl.ds(b * side, side)
            aside = jnp.where(has_left, left_ref[at, :].astype(jnp.float32), 0.0)
            aside += jnp.where(has_right, right_ref[at, :].astype(jnp.float32), 0.0)
            to_mid[pl.ds(inner + b * side, side), :] = aside.astype(jnp.bfloat16)
            mass.append(aside + mid_ref[at, :].astype(jnp.float32))
        top = functools.reduce(jnp.maximum, mass)
        top = jnp.max(top, axis=1, keepdims=True)
        power = jnp.round(jnp.log2(jnp.clip(top, 2.0**-126, 2.0**126)))
        half = half_ref[0:1, 0:1]
        for b in range(own):
            at = pl.ds(b * side, side)
            scaled = (mass[b] * jnp.exp2(-power) * jnp.exp2(-half)).astype(jnp.bfloat16)
            grown = scaled.astype(jnp.float32) / growth_ref[0:1, at]
            src[at, :] = grown.astype(jnp.bfloat16)
        push_forward(rows_ref, cols_ref, src, blk, acc, first_row, first_row - BAND_REACH, copies)
        power_row = as_row(power + half, side)
        to_left[pl.ds(inner, reach), :] = acc[0:reach, :].astype(jnp.bfloat16)
        to_right[pl.ds(inner, reach), :] = acc[reach + inner :, :].astype(jnp.bfloat16)
        keep_ref[...] = acc[reach : reach + inner, :]
        tall = jnp.concatenate([power_row, power_row], axis=0).astype(jnp.bfloat16)
        to_left[pl.ds(inner + reach, 16), :] = tall
        to_right[pl.ds(inner + reach, 16), :] = tall
        total = acc[0:side, :]
        for w in range(1, own + 2 * BAND_REACH):
            total += acc[w * side : (w + 1) * side, :]
        sums = jnp.sum(jnp.transpose(total), axis=0, keepdims=True)
        part_ref[0:8, :] = jnp.broadcast_to(sums, (8, side))
        part_ref[8:16, :] = power_row

        panels = last_ref.shape[0]
        for w in range(own + 2 * BAND_REACH):
            if w < BAND_REACH:
                rows = pl.ds(reach + w * LABEL_ROWS, LABEL_ROWS)
                labels = left_ref[rows, :][0:panels].astype(jnp.float32).astype(jnp.int32)
            elif w < BAND_REACH + own:
                labels = last_ref[:, pl.ds((w - BAND_REACH) * side, side)]
            else:
                rows = pl.ds(reach + (w - BAND_REACH - own) * LABEL_ROWS, LABEL_ROWS)
                labels = right_ref[rows, :][0:panels].astype(jnp.float32).astype(jnp.int32)
            fated[pl.ds(w * side, side), :] = jnp.where(one_hot(labels), 1.0, 0.0).astype(jnp.bfloat16)
        pull_backward(rows_ref, cols_ref, fated, blk, pulled, first_row, first_row - BAND_REACH, None)
        for b in range(own):
            at = pl.ds(b * side, side)
            fates = fates_of(pulled[at, :])
            to_left[at, :] = fates
            to_mid[at, :] = fates
            to_right[at, :] = fates


def third_kernel(own, rows_ref, cols_ref, left_ref, mid_ref, right_ref, mine_ref, blocks_hbm,
                 fate_ref, blk, fated, pulled, sems):
    side = blk.shape[1]
    first_row = lax.axis_index("cell") * own
    reach, inner = BAND_REACH * side, own * side

    @pl.when(lax.axis_index("tm") == 0)
    def _():
        copies = load_blocks(blocks_hbm, blk, sems)
        for copy in copies:
            copy.start()
        fated[0:reach, :] = left_ref[0:reach, :]
        fated[reach : reach + inner, :] = mid_ref[0:inner, :]
        fated[reach + inner :, :] = right_ref[0:reach, :]
        pull_backward(rows_ref, cols_ref, fated, blk, pulled, first_row, first_row - BAND_REACH, copies)
        for b in range(own):
            at = pl.ds(b * side, side)
            fate_ref[0, :, at] = fates_of(pulled[at, :])

    @pl.when(lax.axis_index("tm") != 0)
    def _():
        for b in range(own):
            at = pl.ds(b * side, side)
            fate_ref[0, :, at] = mine_ref[at, :]


def combined(parts):
    top = functools.reduce(jnp.maximum, [part[8:16] for part in parts])
    total = sum(part[0:8] * jnp.exp2(part[8:16] - top) for part in parts)
    return total, top


def last_kernel(own, all_cells, count, *refs):
    part_refs = refs[:count]
    own_part, keep_first, halo_first, keep_second, left_ref, right_ref, mass_ref = refs[count:]
    side = keep_first.shape[1]
    reach, inner = BAND_REACH * side, own * side
    here = lax.axis_index("cell")
    total, top = combined([part[...] for part in part_refs])
    scale = all_cells / as_column(total[0:1], side)

    @pl.when(lax.axis_index("tm") == 0)
    def _():
        for b in range(own):
            at = pl.ds(b * side, side)
            mass = keep_first[at, :] + halo_first[pl.ds(inner + b * side, side), :].astype(jnp.float32)
            mass_ref[0, :, at] = (mass * scale).astype(jnp.bfloat16)

    @pl.when(lax.axis_index("tm") != 0)
    def _():
        has_left, has_right = here > 0, here < lax.axis_size("cell") - 1
        power = pl.ds(inner + reach, 16)
        own_scale = as_column(jnp.exp2(own_part[8:9] - top[0:1]), side)
        left_scale = as_column(jnp.exp2(left_ref[power, :][0:1].astype(jnp.float32) - top[0:1]), side)
        right_scale = as_column(jnp.exp2(right_ref[power, :][0:1].astype(jnp.float32) - top[0:1]), side)
        for b in range(own):
            at = pl.ds(b * side, side)
            aside = pl.ds(inner + b * side, side)
            mass = keep_second[at, :] * own_scale
            mass += jnp.where(has_left, left_ref[aside, :].astype(jnp.float32) * left_scale, 0.0)
            mass += jnp.where(has_right, right_ref[aside, :].astype(jnp.float32) * right_scale, 0.0)
            mass_ref[0, :, at] = (mass * scale).astype(jnp.bfloat16)


def across(array, distance):
    count = lax.axis_size("cell")
    route = []
    for c in range(count):
        there, back = c + distance, c - distance
        route.append((c, count + there if 0 <= there < count else c))
        route.append((count + c, back if 0 <= back < count else count + c))
    return lax.ppermute(array, ("tm", "cell"), route)


def flipped(array, bits):
    return lax.ppermute(array, "cell", [(c, c ^ bits) for c in range(lax.axis_size("cell"))])


def on_device(block_rows, block_cols, block_values, growth, first_labels, last_labels):
    cell_count = lax.axis_size("cell")
    side = block_values.shape[2]
    slots = block_values.shape[1]
    cells = growth.shape[1]
    own = cells // side
    panels = first_labels.shape[0]
    height = panels * CELL_TYPES
    window = own + 2 * BAND_REACH
    reach, inner = BAND_REACH * side, own * side

    smem = pl.BlockSpec(memory_space=pltpu.SMEM)
    vmem = pl.BlockSpec(memory_space=pltpu.VMEM)
    hbm = pl.BlockSpec(memory_space=pl.ANY)
    bf16 = lambda *shape: jax.ShapeDtypeStruct(shape, jnp.bfloat16)
    f32 = lambda *shape: jax.ShapeDtypeStruct(shape, jnp.float32)
    params = pltpu.CompilerParams(vmem_limit_bytes=40 * 1024 * 1024)
    blocks_scratch = pltpu.VMEM((slots, side, side), jnp.bfloat16)
    sems = pltpu.SemaphoreType.DMA((CHUNKS,))

    left, mid, right, keep_first, part, half = pl.pallas_call(
        functools.partial(first_kernel, own),
        out_shape=(
            bf16(reach + own * LABEL_ROWS, side), bf16(inner, side), bf16(reach + own * LABEL_ROWS, side),
            f32(inner, side), f32(16, side), f32(8, side),
        ),
        in_specs=[smem, smem, vmem, vmem, vmem, hbm],
        out_specs=[vmem] * 6,
        scratch_shapes=[
            blocks_scratch, pltpu.VMEM((inner, side), jnp.bfloat16), pltpu.VMEM((window * side, side), jnp.float32), sems,
        ],
        compiler_params=params,
        name="push_first",
    )(block_rows, block_cols, growth, first_labels, last_labels, block_values)

    from_left = across(right, 1)
    from_right = across(left, -1)
    from_mid = across(mid, 0)

    to_left, to_mid, to_right, keep_second, part = pl.pallas_call(
        functools.partial(second_kernel, own),
        out_shape=(
            bf16(inner + reach + 16, side), bf16(2 * inner, side), bf16(inner + reach + 16, side),
            f32(inner, side), f32(16, side),
        ),
        in_specs=[smem, smem] + [vmem] * 7 + [hbm],
        out_specs=[vmem] * 5,
        scratch_shapes=[
            blocks_scratch, pltpu.VMEM((inner, side), jnp.bfloat16), pltpu.VMEM((window * side, side), jnp.float32),
            pltpu.VMEM((window * side, side), jnp.bfloat16), pltpu.VMEM((inner, side), jnp.float32), sems,
        ],
        compiler_params=params,
        name="push_second_pull_first",
    )(block_rows, block_cols, growth, last_labels, from_left, from_mid, from_right, part, half, block_values)

    back_left = across(to_right, -1)
    back_right = across(to_left, 1)
    back_mid = across(to_mid, 0)

    parts = [part]
    bit = 1
    while bit < cell_count:
        if bit > 1:
            total, top = combined(parts)
            parts = [jnp.concatenate([total, top], axis=0)]
        masks = [bit] if 2 * bit >= cell_count else [bit, 2 * bit, 3 * bit]
        parts = [parts[0]] + [flipped(parts[0], mask) for mask in masks]
        bit *= 4

    swap_left = across(back_left, 0)
    swap_right = across(back_right, 0)

    fate = pl.pallas_call(
        functools.partial(third_kernel, own),
        out_shape=bf16(1, height, cells),
        in_specs=[smem, smem] + [vmem] * 4 + [hbm],
        out_specs=vmem,
        scratch_shapes=[
            blocks_scratch, pltpu.VMEM((window * side, side), jnp.bfloat16), pltpu.VMEM((inner, side), jnp.float32), sems,
        ],
        compiler_params=params,
        name="pull_second",
    )(block_rows, block_cols, back_left, back_mid, back_right, to_mid, block_values)

    forward_mass = pl.pallas_call(
        functools.partial(last_kernel, own, float(cells * cell_count), len(parts)),
        out_shape=bf16(1, height, cells),
        in_specs=[vmem] * (len(parts) + 6),
        out_specs=vmem,
        compiler_params=params,
        name="normalise",
    )(*parts, part, keep_first, back_mid, keep_second, swap_left, swap_right)
    return forward_mass, fate


def solution(mesh):
    placed = (
        P("tm", "cell"),
        P("tm", "cell"),
        P("tm", "cell", None, None),
        P("tm", "cell"),
        P(None, "cell"),
        P(None, "cell"),
    )
    return jax.shard_map(
        on_device,
        mesh=mesh,
        in_specs=placed,
        out_specs=(P("tm", None, "cell"), P("tm", None, "cell")),
        check_vma=False,
    )
```

```python
import functools
import jax
import jax.numpy as jnp
from jax import lax
from jax.experimental import pallas as pl
from jax.experimental.pallas import tpu as pltpu
from jax.sharding import PartitionSpec as P

CELL_TYPES = 16
BAND_REACH = 4
LABEL_ROWS = 16
CHUNKS = 8
XA = ((0,), (0,), (0,1))
XB = ((1,), (1,), (0,1))
XC = (0,1)


def rows_of(block, side):
    return pl.ds(pl.multiple_of(block * side, side), side)


def as_column(row, side):
    return jnp.transpose(jnp.broadcast_to(row, (side, side)))


def as_row(column, side):
    return jnp.transpose(jnp.broadcast_to(column, (side, side)))[0:8]


def one_hot(labels):
    types = lax.broadcasted_iota(jnp.int32, (CELL_TYPES, labels.shape[1]), 0)
    return jnp.concatenate([labels[p : p + 1] == types for p in range(labels.shape[0])], axis=0)


def pull_backward(table, src, blk, out, own):
    side = blk.shape[-1]
    per_row = blk.shape[0] // own
    for row in range(own):
        total = None
        for first in range(row * per_row, (row + 1) * per_row, 2):
            slots = [table[0, first], table[0, first + 1]]
            spots = [rows_of(table[1, first], side), rows_of(table[1, first + 1], side)]
            wide = jnp.concatenate([src[spot, :] for spot in spots], axis=1)
            pair = jnp.concatenate([blk[slot] for slot in slots], axis=1)
            pulled = lax.dot_general(wide, pair, (((1,), (1,)), ((), ())), preferred_element_type=jnp.float32)
            total = pulled if total is None else total + pulled
        out[row * side : (row + 1) * side, :] = total


def fates_of(pulled):
    height, cells = pulled.shape
    grouped = pulled.reshape(height // CELL_TYPES, CELL_TYPES, cells)
    scale = CELL_TYPES / jnp.sum(grouped, axis=1, keepdims=True)
    return (grouped * scale).reshape(height, cells).astype(jnp.bfloat16)


def first_kernel(own, rows_hbm, cols_hbm, growth_hbm, first_hbm, last_hbm, blocks_hbm,
                 left_ref, mid_ref, right_ref, keep_ref, part_ref, half_ref, table_hbm, growth, labels, blk,
                 rows, cols, src, acc, count, table, small_sems, sems):
    side = blk.shape[1]
    slots = blk.shape[0]
    first_row = lax.axis_index("cell") * own
    first_col = first_row - BAND_REACH
    on_first = lax.axis_index("tm") == 0
    chunk = slots // CHUNKS
    small = [
        pltpu.make_async_copy(rows_hbm, rows, small_sems.at[0]),
        pltpu.make_async_copy(cols_hbm, cols, small_sems.at[1]),
        pltpu.make_async_copy(growth_hbm, growth, small_sems.at[2]),
        pltpu.make_async_copy(first_hbm, labels.at[0], small_sems.at[3]),
        pltpu.make_async_copy(last_hbm, labels.at[1], small_sems.at[4]),
    ]
    copies = [
        pltpu.make_async_copy(blocks_hbm.at[0, pl.ds(i * chunk, chunk)], blk.at[pl.ds(i * chunk, chunk)], sems.at[i])
        for i in range(CHUNKS)
    ]
    for copy in small + copies:
        copy.start()
    small[0].wait()
    small[1].wait()
    for row in range(own):
        count[row] = row * (slots // own)
    for n in range(slots):
        row = rows[0, n] - first_row
        place = count[row]
        count[row] = place + 1
        table[0, place] = n
        table[1, place] = cols[0, n] - first_col
    table_copy = pltpu.make_async_copy(table, table_hbm, small_sems.at[5])
    table_copy.start()
    for copy in small[2:]:
        copy.wait()

    @pl.when(on_first)
    def _():
        for b in range(own):
            cells = pl.ds(b * side, side)
            inverse = 1.0 / growth[0:1, cells]
            hot = one_hot(labels[0, :, cells])
            src[pl.ds(b * side, side), :] = jnp.where(hot, inverse, 0.0).astype(jnp.bfloat16)
        acc[...] = jnp.zeros_like(acc)
        for n in range(slots):
            if n % chunk == 0:
                copies[n // chunk].wait()
            row = rows_of(rows[0, n] - first_row, side)
            col = rows_of(cols[0, n] - first_col, side)
            acc[col, :] += jnp.dot(src[row, :], blk[n], preferred_element_type=jnp.float32)
        reach = BAND_REACH * side
        inner = own * side
        left_ref[0:reach, :] = acc[0:reach, :].astype(jnp.bfloat16)
        mid_ref[...] = acc[reach : reach + inner, :].astype(jnp.bfloat16)
        right_ref[0:reach, :] = acc[reach + inner :, :].astype(jnp.bfloat16)
        keep_ref[...] = acc[reach : reach + inner, :]
        for b in range(own):
            known = labels[1, :, pl.ds(b * side, side)].astype(jnp.float32).astype(jnp.bfloat16)
            tall = jnp.concatenate([known, known], axis=0)
            left_ref[pl.ds(reach + b * LABEL_ROWS, LABEL_ROWS), :] = tall
            right_ref[pl.ds(reach + b * LABEL_ROWS, LABEL_ROWS), :] = tall
        total = acc[0:side, :]
        for w in range(1, own + 2 * BAND_REACH):
            total += acc[w * side : (w + 1) * side, :]
        sums = jnp.sum(jnp.transpose(total), axis=0, keepdims=True)
        part_ref[0:8, :] = jnp.broadcast_to(sums, (8, side))
        part_ref[8:16, :] = jnp.zeros((8, side), jnp.float32)

    @pl.when(jnp.logical_not(on_first))
    def _():
        for copy in copies:
            copy.wait()
        largest = blk[0].astype(jnp.float32)
        for n in range(1, slots):
            largest = jnp.maximum(largest, blk[n].astype(jnp.float32))
        top = jnp.max(jnp.max(largest, axis=0, keepdims=True), axis=1, keepdims=True)
        half = jnp.round(0.5 * jnp.log2(jnp.maximum(top, 2.0**-126)))
        half_ref[...] = jnp.broadcast_to(half, half_ref.shape)

    table_copy.wait()


def second_kernel(own, table_hbm, growth_ref, labels_ref, left_ref, mid_ref, right_ref, part_in, half_ref, blk,
                  to_left, to_mid, to_right, keep_ref, part_ref, table, src, acc, fated, pulled, sem):
    side = blk.shape[1]
    slots = blk.shape[0]
    here = lax.axis_index("cell")
    reach, inner = BAND_REACH * side, own * side

    @pl.when(lax.axis_index("tm") == 0)
    def _():
        part_ref[...] = part_in[...]

    @pl.when(lax.axis_index("tm") != 0)
    def _():
        table_copy = pltpu.make_async_copy(table_hbm, table, sem)
        table_copy.start()
        has_left, has_right = here > 0, here < lax.axis_size("cell") - 1
        mass = []
        for b in range(own):
            at = pl.ds(b * side, side)
            aside = jnp.where(has_left, left_ref[at, :].astype(jnp.float32), 0.0)
            aside += jnp.where(has_right, right_ref[at, :].astype(jnp.float32), 0.0)
            to_mid[pl.ds(inner + b * side, side), :] = aside.astype(jnp.bfloat16)
            mass.append(aside + mid_ref[at, :].astype(jnp.float32))
        top = functools.reduce(jnp.maximum, mass)
        top = jnp.max(top, axis=1, keepdims=True)
        power = jnp.round(jnp.log2(jnp.clip(top, 2.0**-126, 2.0**126)))
        half = half_ref[0:1, 0:1]
        for b in range(own):
            at = pl.ds(b * side, side)
            scaled = (mass[b] * jnp.exp2(-power) * jnp.exp2(-half)).astype(jnp.bfloat16)
            grown = scaled.astype(jnp.float32) / growth_ref[0:1, at]
            src[at, :] = grown.astype(jnp.bfloat16)
        acc[...] = jnp.zeros_like(acc)
        table_copy.wait()
        for n in range(slots):
            row = n // (slots // own) * side
            col = rows_of(table[1, n], side)
            acc[col, :] += jnp.dot(src[row : row + side, :], blk[table[0, n]], preferred_element_type=jnp.float32)
        power_row = as_row(power + half, side)
        to_left[pl.ds(inner, reach), :] = acc[0:reach, :].astype(jnp.bfloat16)
        to_right[pl.ds(inner, reach), :] = acc[reach + inner :, :].astype(jnp.bfloat16)
        keep_ref[...] = acc[reach : reach + inner, :]
        tall = jnp.concatenate([power_row, power_row], axis=0).astype(jnp.bfloat16)
        to_left[pl.ds(inner + reach, 16), :] = tall
        to_right[pl.ds(inner + reach, 16), :] = tall
        total = acc[0:side, :]
        for w in range(1, own + 2 * BAND_REACH):
            total += acc[w * side : (w + 1) * side, :]
        sums = jnp.sum(jnp.transpose(total), axis=0, keepdims=True)
        part_ref[0:8, :] = jnp.broadcast_to(sums, (8, side))
        part_ref[8:16, :] = power_row

        panels = labels_ref.shape[1]
        for w in range(own + 2 * BAND_REACH):
            if w < BAND_REACH:
                rows = pl.ds(reach + w * LABEL_ROWS, LABEL_ROWS)
                labels = left_ref[rows, :][0:panels].astype(jnp.float32).astype(jnp.int32)
            elif w < BAND_REACH + own:
                labels = labels_ref[1, :, pl.ds((w - BAND_REACH) * side, side)]
            else:
                rows = pl.ds(reach + (w - BAND_REACH - own) * LABEL_ROWS, LABEL_ROWS)
                labels = right_ref[rows, :][0:panels].astype(jnp.float32).astype(jnp.int32)
            fated[pl.ds(w * side, side), :] = jnp.where(one_hot(labels), 1.0, 0.0).astype(jnp.bfloat16)
        pull_backward(table, fated, blk, pulled, own)
        for b in range(own):
            at = pl.ds(b * side, side)
            fates = fates_of(pulled[at, :])
            to_left[at, :] = fates
            to_mid[at, :] = fates
            to_right[at, :] = fates


def third_kernel(own, table_hbm, left_ref, mid_ref, right_ref, mine_ref, blk, fate_ref, table, fated, pulled, sem):
    side = blk.shape[1]
    reach, inner = BAND_REACH * side, own * side

    @pl.when(lax.axis_index("tm") == 0)
    def _():
        table_copy = pltpu.make_async_copy(table_hbm, table, sem)
        table_copy.start()
        fated[0:reach, :] = left_ref[0:reach, :]
        fated[reach : reach + inner, :] = mid_ref[0:inner, :]
        fated[reach + inner :, :] = right_ref[0:reach, :]
        table_copy.wait()
        pull_backward(table, fated, blk, pulled, own)
        for b in range(own):
            at = pl.ds(b * side, side)
            fate_ref[0, :, at] = fates_of(pulled[at, :])

    @pl.when(lax.axis_index("tm") != 0)
    def _():
        for b in range(own):
            at = pl.ds(b * side, side)
            fate_ref[0, :, at] = mine_ref[at, :]


def combined(parts):
    top = functools.reduce(jnp.maximum, [part[8:16] for part in parts])
    total = sum(part[0:8] * jnp.exp2(part[8:16] - top) for part in parts)
    return total, top


def last_kernel(own, all_cells, count, *refs):
    part_refs = refs[:count]
    own_part, keep_first, halo_first, keep_second, left_ref, right_ref, mass_ref = refs[count:]
    side = keep_first.shape[1]
    reach, inner = BAND_REACH * side, own * side
    here = lax.axis_index("cell")
    total, top = combined([part[...] for part in part_refs])
    scale = all_cells / as_column(total[0:1], side)

    @pl.when(lax.axis_index("tm") == 0)
    def _():
        for b in range(own):
            at = pl.ds(b * side, side)
            mass = keep_first[at, :] + halo_first[pl.ds(inner + b * side, side), :].astype(jnp.float32)
            mass_ref[0, :, at] = (mass * scale).astype(jnp.bfloat16)

    @pl.when(lax.axis_index("tm") != 0)
    def _():
        has_left, has_right = here > 0, here < lax.axis_size("cell") - 1
        power = pl.ds(inner + reach, 16)
        own_scale = as_column(jnp.exp2(own_part[8:9] - top[0:1]), side)
        left_scale = as_column(jnp.exp2(left_ref[power, :][0:1].astype(jnp.float32) - top[0:1]), side)
        right_scale = as_column(jnp.exp2(right_ref[power, :][0:1].astype(jnp.float32) - top[0:1]), side)
        for b in range(own):
            at = pl.ds(b * side, side)
            aside = pl.ds(inner + b * side, side)
            mass = keep_second[at, :] * own_scale
            mass += jnp.where(has_left, left_ref[aside, :].astype(jnp.float32) * left_scale, 0.0)
            mass += jnp.where(has_right, right_ref[aside, :].astype(jnp.float32) * right_scale, 0.0)
            mass_ref[0, :, at] = (mass * scale).astype(jnp.bfloat16)


def across(array, distance, ways=(0, 1)):
    count = lax.axis_size("cell")
    route = []
    for c in range(count):
        there, back = c + distance, c - distance
        if 0 in ways and (0 <= there < count or len(ways) == 2):
            route.append((c, count + there if 0 <= there < count else c))
        if 1 in ways and (0 <= back < count or len(ways) == 2):
            route.append((count + c, back if 0 <= back < count else count + c))
    return lax.ppermute(array, ("tm", "cell"), route)


def flipped(array, bits):
    return lax.ppermute(array, "cell", [(c, c ^ bits) for c in range(lax.axis_size("cell"))])


def on_device(block_rows, block_cols, block_values, growth, first_labels, last_labels):
    cell_count = lax.axis_size("cell")
    side = block_values.shape[2]
    slots = block_values.shape[1]
    cells = growth.shape[1]
    own = cells // side
    panels = first_labels.shape[0]
    height = panels * CELL_TYPES
    window = own + 2 * BAND_REACH
    reach, inner = BAND_REACH * side, own * side

    smem = pl.BlockSpec(memory_space=pltpu.SMEM)
    vmem = pl.BlockSpec(memory_space=pltpu.VMEM)
    hbm = pl.BlockSpec(memory_space=pltpu.HBM)
    bf16 = lambda *shape: jax.ShapeDtypeStruct(shape, jnp.bfloat16)
    f32 = lambda *shape: jax.ShapeDtypeStruct(shape, jnp.float32)
    params = pltpu.CompilerParams(vmem_limit_bytes=16 * 1024 * 1024)
    table_scratch = pltpu.SMEM((2, slots), jnp.int32)
    sem = pltpu.SemaphoreType.DMA

    left, mid, right, keep_first, part, half, table, grown, labels, blocks = pl.pallas_call(
        functools.partial(first_kernel, own),
        out_shape=(
            bf16(reach + own * LABEL_ROWS, side), bf16(inner, side), bf16(reach + own * LABEL_ROWS, side),
            f32(inner, side), f32(16, side), f32(8, side), jax.ShapeDtypeStruct((2, slots), jnp.int32),
            f32(1, cells), jax.ShapeDtypeStruct((2, panels, cells), jnp.int32), bf16(slots, side, side),
        ),
        in_specs=[hbm] * 6,
        out_specs=[vmem] * 6 + [hbm] + [vmem] * 3,
        scratch_shapes=[
            pltpu.SMEM((1, slots), jnp.int32), pltpu.SMEM((1, slots), jnp.int32),
            pltpu.VMEM((inner, side), jnp.bfloat16), pltpu.VMEM((window * side, side), jnp.float32),
            pltpu.SMEM((own,), jnp.int32), table_scratch, sem((6,)), sem((CHUNKS,)),
        ],
        compiler_params=params,
        name="push_first",
    )(*[pltpu.with_memory_space_constraint(array, pltpu.HBM) for array in (
        block_rows, block_cols, growth, first_labels, last_labels, block_values
    )])

    from_left = across(right, 1, XA[0])
    from_right = across(left, -1, XA[1])
    from_mid = across(mid, 0, XA[2])

    to_left, to_mid, to_right, keep_second, part = pl.pallas_call(
        functools.partial(second_kernel, own),
        out_shape=(
            bf16(inner + reach + 16, side), bf16(2 * inner, side), bf16(inner + reach + 16, side),
            f32(inner, side), f32(16, side),
        ),
        in_specs=[hbm] + [vmem] * 8,
        out_specs=[vmem] * 5,
        scratch_shapes=[
            table_scratch, pltpu.VMEM((inner, side), jnp.bfloat16), pltpu.VMEM((window * side, side), jnp.float32),
            pltpu.VMEM((window * side, side), jnp.bfloat16), pltpu.VMEM((inner, side), jnp.float32), sem,
        ],
        compiler_params=params,
        name="push_second_pull_first",
    )(table, grown, labels, from_left, from_mid, from_right, part, half, blocks)

    back_left = across(to_right, -1, XB[0])
    back_right = across(to_left, 1, XB[1])
    back_mid = across(to_mid, 0, XB[2])

    parts = [part]
    bit = 1
    while bit < cell_count:
        if bit > 1:
            total, top = combined(parts)
            parts = [jnp.concatenate([total, top], axis=0)]
        masks = [bit] if 2 * bit >= cell_count else [bit, 2 * bit, 3 * bit]
        parts = [parts[0]] + [flipped(parts[0], mask) for mask in masks]
        bit *= 4

    swap_left = across(back_left, 0, XC)
    swap_right = across(back_right, 0, XC)

    fate = pl.pallas_call(
        functools.partial(third_kernel, own),
        out_shape=bf16(1, height, cells),
        in_specs=[hbm] + [vmem] * 5,
        out_specs=vmem,
        scratch_shapes=[
            table_scratch, pltpu.VMEM((window * side, side), jnp.bfloat16), pltpu.VMEM((inner, side), jnp.float32), sem,
        ],
        compiler_params=params,
        name="pull_second",
    )(table, back_left, back_mid, back_right, to_mid, blocks)

    forward_mass = pl.pallas_call(
        functools.partial(last_kernel, own, float(cells * cell_count), len(parts)),
        out_shape=bf16(1, height, cells),
        in_specs=[vmem] * (len(parts) + 6),
        out_specs=vmem,
        compiler_params=params,
        name="normalise",
    )(*parts, part, keep_first, back_mid, keep_second, swap_left, swap_right)
    return forward_mass, fate


def solution(mesh):
    placed = (
        P("tm", "cell"),
        P("tm", "cell"),
        P("tm", "cell", None, None),
        P("tm", "cell"),
        P(None, "cell"),
        P(None, "cell"),
    )
    return jax.shard_map(
        on_device,
        mesh=mesh,
        in_specs=placed,
        out_specs=(P("tm", None, "cell"), P("tm", None, "cell")),
        check_vma=False,
    )
```

```python
import functools
import jax
import jax.numpy as jnp
from jax import lax
from jax.experimental import pallas as pl
from jax.experimental.pallas import tpu as pltpu
from jax.sharding import PartitionSpec as P

CELL_TYPES = 16
BAND_REACH = 4
LABEL_ROWS = 16
CHUNKS = 2
XA = ("inc", "chain", "full")
XB = ("inc", "chain", "full")
XC = "full"


def rows_of(block, side):
    return pl.ds(pl.multiple_of(block * side, side), side)


def as_column(row, side):
    return jnp.transpose(jnp.broadcast_to(row, (side, side)))


def as_row(column, side):
    return jnp.transpose(jnp.broadcast_to(column, (side, side)))[0:8]


def one_hot(labels):
    types = lax.broadcasted_iota(jnp.int32, (CELL_TYPES, labels.shape[1]), 0)
    return jnp.concatenate([labels[p : p + 1] == types for p in range(labels.shape[0])], axis=0)


def pull_backward(table, src, blk, out, own):
    side = blk.shape[-1]
    per_row = blk.shape[0] // own
    for row in range(own):
        total = None
        for first in range(row * per_row, (row + 1) * per_row, 2):
            slots = [table[0, first], table[0, first + 1]]
            spots = [rows_of(table[1, first], side), rows_of(table[1, first + 1], side)]
            wide = jnp.concatenate([src[spot, :] for spot in spots], axis=1)
            pair = jnp.concatenate([blk[slot] for slot in slots], axis=1)
            pulled = lax.dot_general(wide, pair, (((1,), (1,)), ((), ())), preferred_element_type=jnp.float32)
            total = pulled if total is None else total + pulled
        out[row * side : (row + 1) * side, :] = total


def fates_of(pulled):
    height, cells = pulled.shape
    grouped = pulled.reshape(height // CELL_TYPES, CELL_TYPES, cells)
    scale = CELL_TYPES / jnp.sum(grouped, axis=1, keepdims=True)
    return (grouped * scale).reshape(height, cells).astype(jnp.bfloat16)


def load(own, rows_hbm, cols_hbm, growth_hbm, last_hbm, blocks_hbm, growth, known, blk, rows, cols, small_sems, sems):
    chunk = blk.shape[0] // CHUNKS
    small = [
        pltpu.make_async_copy(rows_hbm, rows, small_sems.at[0]),
        pltpu.make_async_copy(cols_hbm, cols, small_sems.at[1]),
        pltpu.make_async_copy(growth_hbm, growth, small_sems.at[2]),
        pltpu.make_async_copy(last_hbm, known, small_sems.at[3]),
    ]
    copies = [
        pltpu.make_async_copy(blocks_hbm.at[0, pl.ds(i * chunk, chunk)], blk.at[pl.ds(i * chunk, chunk)], sems.at[i])
        for i in range(CHUNKS)
    ]
    for copy in small + copies:
        copy.start()
    return small, copies


def sort_slots(own, rows, cols, count, table, first_row):
    slots = table.shape[1]
    for row in range(own):
        count[row] = row * (slots // own)
    for n in range(slots):
        row = rows[0, n] - first_row
        place = count[row]
        count[row] = place + 1
        table[0, place] = n
        table[1, place] = cols[0, n] - first_row + BAND_REACH


def first_kernel(own, rows_hbm, cols_hbm, growth_hbm, first_hbm, last_hbm, blocks_hbm,
                 left_ref, mid_ref, right_ref, keep_ref, part_ref, table_ref, growth, known, blk,
                 rows, cols, labels, src, acc, count, table, small_sems, sems):
    side = blk.shape[1]
    slots = blk.shape[0]
    first_row = lax.axis_index("cell") * own
    reach, inner = BAND_REACH * side, own * side

    @pl.when(lax.axis_index("tm") == 0)
    def _():
        labels_copy = pltpu.make_async_copy(first_hbm, labels, small_sems.at[5])
        labels_copy.start()
        small, copies = load(
            own, rows_hbm, cols_hbm, growth_hbm, last_hbm, blocks_hbm, growth, known, blk, rows, cols, small_sems, sems
        )
        small[0].wait()
        small[1].wait()
        sort_slots(own, rows, cols, count, table, first_row)
        table_copy = pltpu.make_async_copy(table, table_ref, small_sems.at[4])
        table_copy.start()
        small[2].wait()
        small[3].wait()
        labels_copy.wait()
        for b in range(own):
            cells = pl.ds(b * side, side)
            inverse = 1.0 / growth[0:1, cells]
            hot = one_hot(labels[:, cells])
            src[pl.ds(b * side, side), :] = jnp.where(hot, inverse, 0.0).astype(jnp.bfloat16)
        acc[...] = jnp.zeros_like(acc)
        for n in range(slots):
            if n % (slots // CHUNKS) == 0:
                copies[n // (slots // CHUNKS)].wait()
            row = rows_of(rows[0, n] - first_row, side)
            col = rows_of(cols[0, n] - first_row + BAND_REACH, side)
            acc[col, :] += jnp.dot(src[row, :], blk[n], preferred_element_type=jnp.float32)
        left_ref[0:reach, :] = acc[0:reach, :].astype(jnp.bfloat16)
        mid_ref[...] = acc[reach : reach + inner, :].astype(jnp.bfloat16)
        right_ref[0:reach, :] = acc[reach + inner :, :].astype(jnp.bfloat16)
        keep_ref[...] = acc[reach : reach + inner, :]
        for b in range(own):
            exact = known[:, pl.ds(b * side, side)].astype(jnp.float32).astype(jnp.bfloat16)
            tall = jnp.concatenate([exact, exact], axis=0)
            left_ref[pl.ds(reach + b * LABEL_ROWS, LABEL_ROWS), :] = tall
            right_ref[pl.ds(reach + b * LABEL_ROWS, LABEL_ROWS), :] = tall
        total = acc[0:side, :]
        for w in range(1, own + 2 * BAND_REACH):
            total += acc[w * side : (w + 1) * side, :]
        sums = jnp.sum(jnp.transpose(total), axis=0, keepdims=True)
        part_ref[0:8, :] = jnp.broadcast_to(sums, (8, side))
        part_ref[8:16, :] = jnp.zeros((8, side), jnp.float32)
        table_copy.wait()


def prepare_kernel(own, rows_hbm, cols_hbm, growth_hbm, last_hbm, blocks_hbm, table_in, growth_in, known_in, blk_in,
                   table_ref, growth, known, blk, half_ref, rows, cols, count, table, small_sems, sems):
    side = blk.shape[1]
    slots = blk.shape[0]
    first_row = lax.axis_index("cell") * own

    @pl.when(lax.axis_index("tm") != 0)
    def _():
        small, copies = load(
            own, rows_hbm, cols_hbm, growth_hbm, last_hbm, blocks_hbm, growth, known, blk, rows, cols, small_sems, sems
        )
        small[0].wait()
        small[1].wait()
        sort_slots(own, rows, cols, count, table, first_row)
        table_copy = pltpu.make_async_copy(table, table_ref, small_sems.at[4])
        table_copy.start()
        small[2].wait()
        small[3].wait()
        for copy in copies:
            copy.wait()
        largest = blk[0]
        for n in range(1, slots):
            largest = jnp.maximum(largest, blk[n])
        largest = largest.astype(jnp.float32)
        top = jnp.max(jnp.max(largest, axis=0, keepdims=True), axis=1, keepdims=True)
        power = jnp.round(jnp.log2(jnp.clip(top, 2.0**-126, 2.0**126)))
        half_ref[...] = jnp.broadcast_to(jnp.round(0.5 * power), half_ref.shape)
        table_copy.wait()


def second_kernel(own, table_ref, growth_ref, known_ref, left_ref, mid_ref, right_ref, part_in, half_ref, blk,
                  to_left, to_mid, to_right, keep_ref, part_ref, table, src, acc, fated, pulled, sem):
    side = blk.shape[1]
    slots = blk.shape[0]
    here = lax.axis_index("cell")
    reach, inner = BAND_REACH * side, own * side

    @pl.when(lax.axis_index("tm") == 0)
    def _():
        part_ref[...] = part_in[...]

    @pl.when(lax.axis_index("tm") != 0)
    def _():
        table_copy = pltpu.make_async_copy(table_ref, table, sem)
        table_copy.start()
        has_left, has_right = here > 0, here < lax.axis_size("cell") - 1
        mass = []
        for b in range(own):
            at = pl.ds(b * side, side)
            aside = jnp.where(has_left, left_ref[at, :].astype(jnp.float32), 0.0)
            aside += jnp.where(has_right, right_ref[at, :].astype(jnp.float32), 0.0)
            to_mid[pl.ds(inner + b * side, side), :] = aside.astype(jnp.bfloat16)
            mass.append(aside + mid_ref[at, :].astype(jnp.float32))
        top = functools.reduce(jnp.maximum, mass)
        top = jnp.max(top, axis=1, keepdims=True)
        power = jnp.round(jnp.log2(jnp.clip(top, 2.0**-126, 2.0**126)))
        half = half_ref[0:1, 0:1]
        for b in range(own):
            at = pl.ds(b * side, side)
            scaled = (mass[b] * jnp.exp2(-power) * jnp.exp2(-half)).astype(jnp.bfloat16)
            grown = scaled.astype(jnp.float32) / growth_ref[0:1, at]
            src[at, :] = grown.astype(jnp.bfloat16)
        acc[...] = jnp.zeros_like(acc)
        table_copy.wait()
        for n in range(slots):
            row = n // (slots // own) * side
            col = rows_of(table[1, n], side)
            acc[col, :] += jnp.dot(src[row : row + side, :], blk[table[0, n]], preferred_element_type=jnp.float32)
        power_row = as_row(power + half, side)
        to_left[pl.ds(inner, reach), :] = acc[0:reach, :].astype(jnp.bfloat16)
        to_right[pl.ds(inner, reach), :] = acc[reach + inner :, :].astype(jnp.bfloat16)
        keep_ref[...] = acc[reach : reach + inner, :]
        tall = jnp.concatenate([power_row, power_row], axis=0).astype(jnp.bfloat16)
        to_left[pl.ds(inner + reach, 16), :] = tall
        to_right[pl.ds(inner + reach, 16), :] = tall
        total = acc[0:side, :]
        for w in range(1, own + 2 * BAND_REACH):
            total += acc[w * side : (w + 1) * side, :]
        sums = jnp.sum(jnp.transpose(total), axis=0, keepdims=True)
        part_ref[0:8, :] = jnp.broadcast_to(sums, (8, side))
        part_ref[8:16, :] = power_row

        panels = known_ref.shape[0]
        for w in range(own + 2 * BAND_REACH):
            if w < BAND_REACH:
                rows = pl.ds(reach + w * LABEL_ROWS, LABEL_ROWS)
                labels = left_ref[rows, :][0:panels].astype(jnp.float32).astype(jnp.int32)
            elif w < BAND_REACH + own:
                labels = known_ref[:, pl.ds((w - BAND_REACH) * side, side)]
            else:
                rows = pl.ds(reach + (w - BAND_REACH - own) * LABEL_ROWS, LABEL_ROWS)
                labels = right_ref[rows, :][0:panels].astype(jnp.float32).astype(jnp.int32)
            fated[pl.ds(w * side, side), :] = jnp.where(one_hot(labels), 1.0, 0.0).astype(jnp.bfloat16)
        pull_backward(table, fated, blk, pulled, own)
        for b in range(own):
            at = pl.ds(b * side, side)
            fates = fates_of(pulled[at, :])
            to_left[at, :] = fates
            to_mid[at, :] = fates
            to_right[at, :] = fates


def third_kernel(own, table_ref, left_ref, mid_ref, right_ref, mine_ref, blk, fate_ref, table, fated, pulled, sem):
    side = blk.shape[1]
    reach, inner = BAND_REACH * side, own * side

    @pl.when(lax.axis_index("tm") == 0)
    def _():
        table_copy = pltpu.make_async_copy(table_ref, table, sem)
        table_copy.start()
        fated[0:reach, :] = left_ref[0:reach, :]
        fated[reach : reach + inner, :] = mid_ref[0:inner, :]
        fated[reach + inner :, :] = right_ref[0:reach, :]
        table_copy.wait()
        pull_backward(table, fated, blk, pulled, own)
        for b in range(own):
            at = pl.ds(b * side, side)
            fate_ref[0, :, at] = fates_of(pulled[at, :])

    @pl.when(lax.axis_index("tm") != 0)
    def _():
        for b in range(own):
            at = pl.ds(b * side, side)
            fate_ref[0, :, at] = mine_ref[at, :]


def combined(parts):
    top = functools.reduce(jnp.maximum, [part[8:16] for part in parts])
    total = sum(part[0:8] * jnp.exp2(part[8:16] - top) for part in parts)
    return total, top


def combine_kernel(count, *refs):
    total, top = combined([part[...] for part in refs[:count]])
    out = refs[count + 2]
    out[0:8, :] = total
    out[8:16, :] = top


def last_kernel(own, all_cells, whole, own_part, keep_first, halo_first, keep_second, left_ref, right_ref, mass_ref):
    side = keep_first.shape[1]
    reach, inner = BAND_REACH * side, own * side
    here = lax.axis_index("cell")
    total, top = whole[0:8, :], whole[8:16, :]
    scale = all_cells / as_column(total[0:1], side)

    @pl.when(lax.axis_index("tm") == 0)
    def _():
        for b in range(own):
            at = pl.ds(b * side, side)
            mass = keep_first[at, :] + halo_first[pl.ds(inner + b * side, side), :].astype(jnp.float32)
            mass_ref[0, :, at] = (mass * scale).astype(jnp.bfloat16)

    @pl.when(lax.axis_index("tm") != 0)
    def _():
        has_left, has_right = here > 0, here < lax.axis_size("cell") - 1
        power = pl.ds(inner + reach, 16)
        own_scale = as_column(jnp.exp2(own_part[8:9] - top[0:1]), side)
        left_scale = as_column(jnp.exp2(left_ref[power, :][0:1].astype(jnp.float32) - top[0:1]), side)
        right_scale = as_column(jnp.exp2(right_ref[power, :][0:1].astype(jnp.float32) - top[0:1]), side)
        for b in range(own):
            at = pl.ds(b * side, side)
            aside = pl.ds(inner + b * side, side)
            mass = keep_second[at, :] * own_scale
            mass += jnp.where(has_left, left_ref[aside, :].astype(jnp.float32) * left_scale, 0.0)
            mass += jnp.where(has_right, right_ref[aside, :].astype(jnp.float32) * right_scale, 0.0)
            mass_ref[0, :, at] = (mass * scale).astype(jnp.bfloat16)


def across(array, distance, sender, mode):
    count = lax.axis_size("cell")
    at = lambda core, c: core * count + c
    other = 1 - sender
    route = {at(sender, c): at(other, c + distance) for c in range(count) if 0 <= c + distance < count}
    if mode == "full":
        for c in range(count):
            route[at(other, c)] = at(sender, c - distance) if 0 <= c - distance < count else at(other, c)
            route.setdefault(at(sender, c), at(sender, c))
    if mode == "chain":
        for c in range(count):
            route[at(other, c)] = at(sender, c)
            route.setdefault(at(sender, c), at(other, (c + distance) % count))
    return lax.ppermute(array, ("tm", "cell"), list(route.items()))


def flipped(array, bits):
    return lax.ppermute(array, "cell", [(c, c ^ bits) for c in range(lax.axis_size("cell"))])


def on_device(block_rows, block_cols, block_values, growth, first_labels, last_labels):
    cell_count = lax.axis_size("cell")
    side = block_values.shape[2]
    slots = block_values.shape[1]
    cells = growth.shape[1]
    own = cells // side
    panels = first_labels.shape[0]
    height = panels * CELL_TYPES
    window = own + 2 * BAND_REACH
    reach, inner = BAND_REACH * side, own * side

    vmem = pl.BlockSpec(memory_space=pltpu.VMEM)
    hbm = pl.BlockSpec(memory_space=pltpu.HBM)
    anywhere = pl.BlockSpec(memory_space=pl.ANY)
    bf16 = lambda *shape: jax.ShapeDtypeStruct(shape, jnp.bfloat16)
    f32 = lambda *shape: jax.ShapeDtypeStruct(shape, jnp.float32)
    i32 = lambda *shape: jax.ShapeDtypeStruct(shape, jnp.int32)
    params = pltpu.CompilerParams(vmem_limit_bytes=16 * 1024 * 1024)
    sem = pltpu.SemaphoreType.DMA
    slot_scratch = [pltpu.SMEM((1, slots), jnp.int32), pltpu.SMEM((1, slots), jnp.int32)]
    sort_scratch = [pltpu.SMEM((own,), jnp.int32), pltpu.SMEM((2, slots), jnp.int32)]
    loaded = (i32(2, slots), f32(1, cells), i32(panels, cells), bf16(slots, side, side))
    inputs = [pltpu.with_memory_space_constraint(array, pltpu.HBM) for array in (
        block_rows, block_cols, growth, first_labels, last_labels, block_values
    )]

    left, mid, right, keep_first, part, *loads = pl.pallas_call(
        functools.partial(first_kernel, own),
        out_shape=(
            bf16(reach + own * LABEL_ROWS, side), bf16(inner, side), bf16(reach + own * LABEL_ROWS, side), f32(inner, side),
            f32(16, side), *loaded,
        ),
        in_specs=[hbm] * 6,
        out_specs=[vmem] * 9,
        scratch_shapes=slot_scratch + [
            pltpu.VMEM((panels, cells), jnp.int32), pltpu.VMEM((inner, side), jnp.bfloat16),
            pltpu.VMEM((window * side, side), jnp.float32),
        ] + sort_scratch + [sem((6,)), sem((CHUNKS,))],
        compiler_params=params,
        name="push_first",
    )(*inputs)

    from_left = across(right, 1, 0, XA[0])
    from_right = across(left, -1, 0, XA[1])
    from_mid = across(mid, 0, 0, XA[2])

    table, rates, known, blocks, half = pl.pallas_call(
        functools.partial(prepare_kernel, own),
        out_shape=loaded + (f32(8, side),),
        in_specs=[hbm] * 5 + [vmem] * 4,
        out_specs=[vmem] * 5,
        scratch_shapes=slot_scratch + sort_scratch + [sem((6,)), sem((CHUNKS,))],
        input_output_aliases={5 + i: i for i in range(4)},
        compiler_params=params,
        name="prepare",
    )(*inputs[:3], *inputs[4:], *loads)

    to_left, to_mid, to_right, keep_second, part = pl.pallas_call(
        functools.partial(second_kernel, own),
        out_shape=(
            bf16(inner + reach + 16, side), bf16(2 * inner, side), bf16(inner + reach + 16, side),
            f32(inner, side), f32(16, side),
        ),
        in_specs=[vmem] * 9,
        out_specs=[vmem] * 5,
        scratch_shapes=[
            pltpu.SMEM((2, slots), jnp.int32), pltpu.VMEM((inner, side), jnp.bfloat16), pltpu.VMEM((window * side, side), jnp.float32),
            pltpu.VMEM((window * side, side), jnp.bfloat16), pltpu.VMEM((inner, side), jnp.float32), sem,
        ],
        compiler_params=params,
        name="push_second_pull_first",
    )(table, rates, known, from_left, from_mid, from_right, part, half, blocks)

    back_left = across(to_right, 1, 1, XB[0])
    back_right = across(to_left, -1, 1, XB[1])
    back_mid = across(to_mid, 0, 1, XB[2])

    whole = part
    bit = 1
    while bit < cell_count:
        if bit > 1:
            whole = jnp.concatenate(combined(parts), axis=0)
        parts = [whole] + [flipped(whole, k * bit) for k in range(1, 4) if k * bit < cell_count]
        bit *= 4
    whole, back_left, back_right = pl.pallas_call(
        functools.partial(combine_kernel, len(parts)),
        out_shape=(f32(16, side), bf16(inner + reach + 16, side), bf16(inner + reach + 16, side)),
        in_specs=[vmem] * len(parts) + [anywhere] * 2,
        out_specs=[vmem] + [anywhere] * 2,
        input_output_aliases={len(parts): 1, len(parts) + 1: 2},
        compiler_params=params,
        name="combine",
    )(*parts, back_left, back_right)

    swap_left = across(back_left, 0, 0, XC)
    swap_right = across(back_right, 0, 0, XC)

    fate = pl.pallas_call(
        functools.partial(third_kernel, own),
        out_shape=bf16(1, height, cells),
        in_specs=[vmem] * 6,
        out_specs=vmem,
        scratch_shapes=[
            pltpu.SMEM((2, slots), jnp.int32), pltpu.VMEM((window * side, side), jnp.bfloat16), pltpu.VMEM((inner, side), jnp.float32), sem,
        ],
        compiler_params=params,
        name="pull_second",
    )(table, back_left, back_mid, back_right, to_mid, blocks)

    forward_mass = pl.pallas_call(
        functools.partial(last_kernel, own, float(cells * cell_count)),
        out_shape=bf16(1, height, cells),
        in_specs=[vmem] * 7,
        out_specs=vmem,
        compiler_params=params,
        name="normalise",
    )(whole, part, keep_first, back_mid, keep_second, swap_left, swap_right)
    return forward_mass, fate


def solution(mesh):
    placed = (
        P("tm", "cell"),
        P("tm", "cell"),
        P("tm", "cell", None, None),
        P("tm", "cell"),
        P(None, "cell"),
        P(None, "cell"),
    )
    return jax.shard_map(
        on_device,
        mesh=mesh,
        in_specs=placed,
        out_specs=(P("tm", None, "cell"), P("tm", None, "cell")),
        check_vma=False,
    )
```

```python
import functools
import jax
import jax.numpy as jnp
from jax import lax
from jax.experimental import pallas as pl
from jax.experimental.pallas import tpu as pltpu
from jax.sharding import PartitionSpec as P

CELL_TYPES = 16
BAND_REACH = 4
LABEL_ROWS = 16
CHUNKS = 2
XA = ("inc", "chain", "full")
XB = ("inc", "chain", "full")
XC = "full"


def rows_of(block, side):
    return pl.ds(pl.multiple_of(block * side, side), side)


def as_column(row, side):
    return jnp.transpose(jnp.broadcast_to(row, (side, side)))


def as_row(column, side):
    return jnp.transpose(jnp.broadcast_to(column, (side, side)))[0:8]


def one_hot(labels):
    types = lax.broadcasted_iota(jnp.int32, (CELL_TYPES, labels.shape[1]), 0)
    return jnp.concatenate([labels[p : p + 1] == types for p in range(labels.shape[0])], axis=0)


def pull_backward(table, src, blk, out, own):
    side = blk.shape[-1]
    per_row = blk.shape[0] // own
    for row in range(own):
        total = None
        for first in range(row * per_row, (row + 1) * per_row, 2):
            slots = [table[0, first], table[0, first + 1]]
            spots = [rows_of(table[1, first], side), rows_of(table[1, first + 1], side)]
            wide = jnp.concatenate([src[spot, :] for spot in spots], axis=1)
            pair = jnp.concatenate([blk[slot] for slot in slots], axis=1)
            pulled = lax.dot_general(wide, pair, (((1,), (1,)), ((), ())), preferred_element_type=jnp.float32)
            total = pulled if total is None else total + pulled
        out[row * side : (row + 1) * side, :] = total


def labels_of(sent, start, block, panels):
    tile = sent[pl.ds(start + block // 2 * LABEL_ROWS, LABEL_ROWS), :].astype(jnp.float32).astype(jnp.int32)
    return tile[block % 2 * panels : (block % 2 + 1) * panels]


def fates_of(pulled):
    height, cells = pulled.shape
    grouped = pulled.reshape(height // CELL_TYPES, CELL_TYPES, cells)
    scale = CELL_TYPES / jnp.sum(grouped, axis=1, keepdims=True)
    return (grouped * scale).reshape(height, cells).astype(jnp.bfloat16)


def load(own, rows_hbm, cols_hbm, growth_hbm, last_hbm, blocks_hbm, growth, known, blk, rows, cols, small_sems, sems):
    chunk = blk.shape[0] // CHUNKS
    small = [
        pltpu.make_async_copy(rows_hbm, rows, small_sems.at[0]),
        pltpu.make_async_copy(cols_hbm, cols, small_sems.at[1]),
        pltpu.make_async_copy(growth_hbm, growth, small_sems.at[2]),
        pltpu.make_async_copy(last_hbm, known, small_sems.at[3]),
    ]
    copies = [
        pltpu.make_async_copy(blocks_hbm.at[0, pl.ds(i * chunk, chunk)], blk.at[pl.ds(i * chunk, chunk)], sems.at[i])
        for i in range(CHUNKS)
    ]
    for copy in small + copies:
        copy.start()
    return small, copies


def sort_slots(own, rows, cols, count, table, first_row):
    slots = table.shape[1]
    for row in range(own):
        count[row] = row * (slots // own)
    for n in range(slots):
        row = rows[0, n] - first_row
        place = count[row]
        count[row] = place + 1
        table[0, place] = n
        table[1, place] = cols[0, n] - first_row + BAND_REACH


def first_kernel(own, rows_hbm, cols_hbm, growth_hbm, first_hbm, last_hbm, blocks_hbm,
                 left_ref, mid_ref, right_ref, keep_ref, part_ref, table_ref, growth, known, blk,
                 rows, cols, labels, src, acc, count, table, small_sems, sems):
    side = blk.shape[1]
    slots = blk.shape[0]
    first_row = lax.axis_index("cell") * own
    reach, inner = BAND_REACH * side, own * side

    @pl.when(lax.axis_index("tm") == 0)
    def _():
        labels_copy = pltpu.make_async_copy(first_hbm, labels, small_sems.at[5])
        labels_copy.start()
        small, copies = load(
            own, rows_hbm, cols_hbm, growth_hbm, last_hbm, blocks_hbm, growth, known, blk, rows, cols, small_sems, sems
        )
        small[0].wait()
        small[1].wait()
        sort_slots(own, rows, cols, count, table, first_row)
        table_copy = pltpu.make_async_copy(table, table_ref, small_sems.at[4])
        table_copy.start()
        small[2].wait()
        small[3].wait()
        labels_copy.wait()
        for b in range(own):
            cells = pl.ds(b * side, side)
            inverse = 1.0 / growth[0:1, cells]
            hot = one_hot(labels[:, cells])
            src[pl.ds(b * side, side), :] = jnp.where(hot, inverse, 0.0).astype(jnp.bfloat16)
        acc[...] = jnp.zeros_like(acc)
        for n in range(slots):
            if n % (slots // CHUNKS) == 0:
                copies[n // (slots // CHUNKS)].wait()
            row = rows_of(rows[0, n] - first_row, side)
            col = rows_of(cols[0, n] - first_row + BAND_REACH, side)
            acc[col, :] += jnp.dot(src[row, :], blk[n], preferred_element_type=jnp.float32)
        left_ref[0:reach, :] = acc[0:reach, :].astype(jnp.bfloat16)
        mid_ref[...] = acc[reach : reach + inner, :].astype(jnp.bfloat16)
        right_ref[0:reach, :] = acc[reach + inner :, :].astype(jnp.bfloat16)
        keep_ref[...] = acc[reach : reach + inner, :]
        for b in range(0, own, 2):
            pair = [known[:, pl.ds((b + i) * side, side)] for i in range(2)]
            tall = jnp.concatenate(pair, axis=0).astype(jnp.float32).astype(jnp.bfloat16)
            left_ref[pl.ds(reach + b * LABEL_ROWS // 2, LABEL_ROWS), :] = tall
            right_ref[pl.ds(reach + b * LABEL_ROWS // 2, LABEL_ROWS), :] = tall
        total = acc[0:side, :]
        for w in range(1, own + 2 * BAND_REACH):
            total += acc[w * side : (w + 1) * side, :]
        sums = jnp.sum(jnp.transpose(total), axis=0, keepdims=True)
        part_ref[0:8, :] = jnp.broadcast_to(sums, (8, side))
        part_ref[8:16, :] = jnp.zeros((8, side), jnp.float32)
        table_copy.wait()


def prepare_kernel(own, rows_hbm, cols_hbm, growth_hbm, last_hbm, blocks_hbm, table_in, growth_in, known_in, blk_in,
                   table_ref, growth, known, blk, half_ref, rows, cols, count, table, small_sems, sems):
    side = blk.shape[1]
    slots = blk.shape[0]
    first_row = lax.axis_index("cell") * own

    @pl.when(lax.axis_index("tm") != 0)
    def _():
        small, copies = load(
            own, rows_hbm, cols_hbm, growth_hbm, last_hbm, blocks_hbm, growth, known, blk, rows, cols, small_sems, sems
        )
        small[0].wait()
        small[1].wait()
        sort_slots(own, rows, cols, count, table, first_row)
        table_copy = pltpu.make_async_copy(table, table_ref, small_sems.at[4])
        table_copy.start()
        small[2].wait()
        small[3].wait()
        for copy in copies:
            copy.wait()
        largest = blk[0]
        for n in range(1, slots):
            largest = jnp.maximum(largest, blk[n])
        largest = largest.astype(jnp.float32)
        top = jnp.max(jnp.max(largest, axis=0, keepdims=True), axis=1, keepdims=True)
        power = jnp.round(jnp.log2(jnp.clip(top, 2.0**-126, 2.0**126)))
        half_ref[...] = jnp.broadcast_to(jnp.round(0.5 * power), half_ref.shape)
        table_copy.wait()


def second_kernel(own, table_ref, growth_ref, known_ref, left_ref, mid_ref, right_ref, part_in, half_ref, blk,
                  to_left, to_mid, to_right, keep_ref, part_ref, table, src, acc, fated, pulled, sem):
    side = blk.shape[1]
    slots = blk.shape[0]
    here = lax.axis_index("cell")
    reach, inner = BAND_REACH * side, own * side

    @pl.when(lax.axis_index("tm") == 0)
    def _():
        part_ref[...] = part_in[...]

    @pl.when(lax.axis_index("tm") != 0)
    def _():
        table_copy = pltpu.make_async_copy(table_ref, table, sem)
        table_copy.start()
        has_left, has_right = here > 0, here < lax.axis_size("cell") - 1
        mass = []
        for b in range(own):
            at = pl.ds(b * side, side)
            aside = jnp.where(has_left, left_ref[at, :].astype(jnp.float32), 0.0)
            aside += jnp.where(has_right, right_ref[at, :].astype(jnp.float32), 0.0)
            to_mid[pl.ds(inner + b * side, side), :] = aside.astype(jnp.bfloat16)
            mass.append(aside + mid_ref[at, :].astype(jnp.float32))
        top = functools.reduce(jnp.maximum, mass)
        top = jnp.max(top, axis=1, keepdims=True)
        power = jnp.round(jnp.log2(jnp.clip(top, 2.0**-126, 2.0**126)))
        half = half_ref[0:1, 0:1]
        for b in range(own):
            at = pl.ds(b * side, side)
            scaled = (mass[b] * jnp.exp2(-power) * jnp.exp2(-half)).astype(jnp.bfloat16)
            grown = scaled.astype(jnp.float32) / growth_ref[0:1, at]
            src[at, :] = grown.astype(jnp.bfloat16)
        acc[...] = jnp.zeros_like(acc)
        table_copy.wait()
        for n in range(slots):
            row = n // (slots // own) * side
            col = rows_of(table[1, n], side)
            acc[col, :] += jnp.dot(src[row : row + side, :], blk[table[0, n]], preferred_element_type=jnp.float32)
        power_row = as_row(power + half, side)
        to_left[pl.ds(inner, reach), :] = acc[0:reach, :].astype(jnp.bfloat16)
        to_right[pl.ds(inner, reach), :] = acc[reach + inner :, :].astype(jnp.bfloat16)
        keep_ref[...] = acc[reach : reach + inner, :]
        tall = jnp.concatenate([power_row, power_row], axis=0).astype(jnp.bfloat16)
        to_left[pl.ds(inner + reach, 16), :] = tall
        to_right[pl.ds(inner + reach, 16), :] = tall
        total = acc[0:side, :]
        for w in range(1, own + 2 * BAND_REACH):
            total += acc[w * side : (w + 1) * side, :]
        sums = jnp.sum(jnp.transpose(total), axis=0, keepdims=True)
        part_ref[0:8, :] = jnp.broadcast_to(sums, (8, side))
        part_ref[8:16, :] = power_row

        panels = known_ref.shape[0]
        for w in range(own + 2 * BAND_REACH):
            if w < BAND_REACH:
                labels = labels_of(left_ref, reach, w, panels)
            elif w < BAND_REACH + own:
                labels = known_ref[:, pl.ds((w - BAND_REACH) * side, side)]
            else:
                labels = labels_of(right_ref, reach, w - BAND_REACH - own, panels)
            fated[pl.ds(w * side, side), :] = jnp.where(one_hot(labels), 1.0, 0.0).astype(jnp.bfloat16)
        pull_backward(table, fated, blk, pulled, own)
        for b in range(own):
            at = pl.ds(b * side, side)
            fates = fates_of(pulled[at, :])
            to_left[at, :] = fates
            to_mid[at, :] = fates
            to_right[at, :] = fates


def combined(parts):
    top = functools.reduce(jnp.maximum, [part[8:16] for part in parts])
    total = sum(part[0:8] * jnp.exp2(part[8:16] - top) for part in parts)
    return total, top


def combine_kernel(count, *refs):
    mine, out, to_swap, sem = refs[count], refs[count + 3], refs[count + 4], refs[count + 6]
    copy = pltpu.make_async_copy(mine, to_swap.at[pl.ds(0, mine.shape[0])], sem)

    @pl.when(lax.axis_index("tm") != 0)
    def _():
        copy.start()

    total, top = combined([part[...] for part in refs[:count]])
    out[0:8, :] = total
    out[8:16, :] = top

    @pl.when(lax.axis_index("tm") != 0)
    def _():
        copy.wait()


def last_kernel(own, all_cells, table_ref, whole, own_part, keep_first, keep_second, back_left, back_right, swap_left,
                swap_right, mine_ref, blk, mass_ref, fate_ref, table, fated, pulled, sem):
    side = blk.shape[1]
    reach, inner = BAND_REACH * side, own * side
    here = lax.axis_index("cell")
    total, top = whole[0:8, :], whole[8:16, :]

    @pl.when(lax.axis_index("tm") == 0)
    def _():
        table_copy = pltpu.make_async_copy(table_ref, table, sem)
        table_copy.start()
        fated[0:reach, :] = back_left[0:reach, :]
        fated[reach : reach + inner, :] = swap_left[0:inner, :]
        fated[reach + inner :, :] = back_right[0:reach, :]
        scale = all_cells / as_column(total[0:1], side)
        for b in range(own):
            at = pl.ds(b * side, side)
            mass = keep_first[at, :] + swap_left[pl.ds(inner + b * side, side), :].astype(jnp.float32)
            mass_ref[0, :, at] = (mass * scale).astype(jnp.bfloat16)
        table_copy.wait()
        pull_backward(table, fated, blk, pulled, own)
        for b in range(own):
            at = pl.ds(b * side, side)
            fate_ref[0, :, at] = fates_of(pulled[at, :])

    @pl.when(lax.axis_index("tm") != 0)
    def _():
        has_left, has_right = here > 0, here < lax.axis_size("cell") - 1
        power = pl.ds(inner + reach, 16)
        scale = all_cells / as_column(total[0:1], side)
        own_scale = as_column(jnp.exp2(own_part[8:9] - top[0:1]), side)
        left_scale = as_column(jnp.exp2(swap_left[power, :][0:1].astype(jnp.float32) - top[0:1]), side)
        right_scale = as_column(jnp.exp2(swap_right[power, :][0:1].astype(jnp.float32) - top[0:1]), side)
        for b in range(own):
            at = pl.ds(b * side, side)
            aside = pl.ds(inner + b * side, side)
            mass = keep_second[at, :] * own_scale
            mass += jnp.where(has_left, swap_left[aside, :].astype(jnp.float32) * left_scale, 0.0)
            mass += jnp.where(has_right, swap_right[aside, :].astype(jnp.float32) * right_scale, 0.0)
            mass_ref[0, :, at] = (mass * scale).astype(jnp.bfloat16)
            fate_ref[0, :, at] = mine_ref[at, :]


def across(array, distance, sender, mode):
    count = lax.axis_size("cell")
    at = lambda core, c: core * count + c
    other = 1 - sender
    route = {at(sender, c): at(other, c + distance) for c in range(count) if 0 <= c + distance < count}
    if mode == "full":
        for c in range(count):
            route[at(other, c)] = at(sender, c - distance) if 0 <= c - distance < count else at(other, c)
            route.setdefault(at(sender, c), at(sender, c))
    if mode == "chain":
        for c in range(count):
            route[at(other, c)] = at(sender, c)
            route.setdefault(at(sender, c), at(other, (c + distance) % count))
    return lax.ppermute(array, ("tm", "cell"), list(route.items()))


def flipped(array, bits):
    return lax.ppermute(array, "cell", [(c, c ^ bits) for c in range(lax.axis_size("cell"))])


def on_device(block_rows, block_cols, block_values, growth, first_labels, last_labels):
    cell_count = lax.axis_size("cell")
    side = block_values.shape[2]
    slots = block_values.shape[1]
    cells = growth.shape[1]
    own = cells // side
    panels = first_labels.shape[0]
    height = panels * CELL_TYPES
    window = own + 2 * BAND_REACH
    reach, inner = BAND_REACH * side, own * side

    vmem = pl.BlockSpec(memory_space=pltpu.VMEM)
    hbm = pl.BlockSpec(memory_space=pltpu.HBM)
    anywhere = pl.BlockSpec(memory_space=pl.ANY)
    bf16 = lambda *shape: jax.ShapeDtypeStruct(shape, jnp.bfloat16)
    f32 = lambda *shape: jax.ShapeDtypeStruct(shape, jnp.float32)
    i32 = lambda *shape: jax.ShapeDtypeStruct(shape, jnp.int32)
    params = pltpu.CompilerParams(vmem_limit_bytes=16 * 1024 * 1024)
    sem = pltpu.SemaphoreType.DMA
    slot_scratch = [pltpu.SMEM((1, slots), jnp.int32), pltpu.SMEM((1, slots), jnp.int32)]
    sort_scratch = [pltpu.SMEM((own,), jnp.int32), pltpu.SMEM((2, slots), jnp.int32)]
    loaded = (i32(2, slots), f32(1, cells), i32(panels, cells), bf16(slots, side, side))
    inputs = [pltpu.with_memory_space_constraint(array, pltpu.HBM) for array in (
        block_rows, block_cols, growth, first_labels, last_labels, block_values
    )]

    left, mid, right, keep_first, part, *loads = pl.pallas_call(
        functools.partial(first_kernel, own),
        out_shape=(
            bf16(reach + own * LABEL_ROWS // 2, side), bf16(inner, side), bf16(reach + own * LABEL_ROWS // 2, side), f32(inner, side),
            f32(16, side), *loaded,
        ),
        in_specs=[hbm] * 6,
        out_specs=[vmem] * 9,
        scratch_shapes=slot_scratch + [
            pltpu.VMEM((panels, cells), jnp.int32), pltpu.VMEM((inner, side), jnp.bfloat16),
            pltpu.VMEM((window * side, side), jnp.float32),
        ] + sort_scratch + [sem((6,)), sem((CHUNKS,))],
        compiler_params=params,
        name="push_first",
    )(*inputs)

    from_left = across(right, 1, 0, XA[0])
    from_right = across(left, -1, 0, XA[1])
    from_mid = across(mid, 0, 0, XA[2])

    table, rates, known, blocks, half = pl.pallas_call(
        functools.partial(prepare_kernel, own),
        out_shape=loaded + (f32(8, side),),
        in_specs=[hbm] * 5 + [vmem] * 4,
        out_specs=[vmem] * 5,
        scratch_shapes=slot_scratch + sort_scratch + [sem((6,)), sem((CHUNKS,))],
        input_output_aliases={5 + i: i for i in range(4)},
        compiler_params=params,
        name="prepare",
    )(*inputs[:3], *inputs[4:], *loads)

    to_left, to_mid, to_right, keep_second, part = pl.pallas_call(
        functools.partial(second_kernel, own),
        out_shape=(
            bf16(inner + reach + 16, side), bf16(2 * inner, side), bf16(inner + reach + 16, side),
            f32(inner, side), f32(16, side),
        ),
        in_specs=[vmem] * 9,
        out_specs=[vmem] * 5,
        scratch_shapes=[
            pltpu.SMEM((2, slots), jnp.int32), pltpu.VMEM((inner, side), jnp.bfloat16), pltpu.VMEM((window * side, side), jnp.float32),
            pltpu.VMEM((window * side, side), jnp.bfloat16), pltpu.VMEM((inner, side), jnp.float32), sem,
        ],
        compiler_params=params,
        name="push_second_pull_first",
    )(table, rates, known, from_left, from_mid, from_right, part, half, blocks)

    back_left = across(to_right, 1, 1, XB[0])
    back_right = across(to_left, -1, 1, XB[1])

    whole = part
    bit = 1
    while bit < cell_count:
        if bit > 1:
            whole = jnp.concatenate(combined(parts), axis=0)
        parts = [whole] + [flipped(whole, k * bit) for k in range(1, 4) if k * bit < cell_count]
        bit *= 4
    whole, back_left, back_right = pl.pallas_call(
        functools.partial(combine_kernel, len(parts)),
        out_shape=(f32(16, side), bf16(inner + reach + 16, side), bf16(inner + reach + 16, side)),
        in_specs=[vmem] * len(parts) + [anywhere] * 3,
        out_specs=[vmem] + [anywhere] * 2,
        scratch_shapes=[sem],
        input_output_aliases={len(parts) + 1: 1, len(parts) + 2: 2},
        compiler_params=params,
        name="combine",
    )(*parts, to_mid, back_left, back_right)

    swap_left = across(back_left, 0, 0, XC)
    swap_right = across(back_right, 0, 0, XC)

    forward_mass, fate = pl.pallas_call(
        functools.partial(last_kernel, own, float(cells * cell_count)),
        out_shape=(bf16(1, height, cells), bf16(1, height, cells)),
        in_specs=[vmem] * 11,
        out_specs=[vmem] * 2,
        scratch_shapes=[
            pltpu.SMEM((2, slots), jnp.int32), pltpu.VMEM((window * side, side), jnp.bfloat16),
            pltpu.VMEM((inner, side), jnp.float32), sem,
        ],
        compiler_params=params,
        name="pull_second_normalise",
    )(table, whole, part, keep_first, keep_second, back_left, back_right, swap_left, swap_right, to_mid, blocks)
    return forward_mass, fate


def solution(mesh):
    placed = (
        P("tm", "cell"),
        P("tm", "cell"),
        P("tm", "cell", None, None),
        P("tm", "cell"),
        P(None, "cell"),
        P(None, "cell"),
    )
    return jax.shard_map(
        on_device,
        mesh=mesh,
        in_specs=placed,
        out_specs=(P("tm", None, "cell"), P("tm", None, "cell")),
        check_vma=False,
    )
```

```python
import functools
import jax
import jax.numpy as jnp
from jax import lax
from jax.experimental import pallas as pl
from jax.experimental.pallas import tpu as pltpu
from jax.sharding import PartitionSpec as P

CELL_TYPES = 16
BAND_REACH = 4
LABEL_ROWS = 16
CHUNKS = 2


def rows_of(block, side):
    return pl.ds(pl.multiple_of(block * side, side), side)


def as_column(row, side):
    return jnp.transpose(jnp.broadcast_to(row, (side, side)))


def as_row(column, side):
    return jnp.transpose(jnp.broadcast_to(column, (side, side)))[0:8]


def one_hot(labels):
    types = lax.broadcasted_iota(jnp.int32, (CELL_TYPES, labels.shape[1]), 0)
    return jnp.concatenate([labels[p : p + 1] == types for p in range(labels.shape[0])], axis=0)


def pull_backward(table, src, blk, out, own):
    side = blk.shape[-1]
    per_row = blk.shape[0] // own
    for row in range(own):
        total = None
        for first in range(row * per_row, (row + 1) * per_row, 2):
            slots = [table[0, first], table[0, first + 1]]
            spots = [rows_of(table[1, first], side), rows_of(table[1, first + 1], side)]
            wide = jnp.concatenate([src[spot, :] for spot in spots], axis=1)
            pair = jnp.concatenate([blk[slot] for slot in slots], axis=1)
            pulled = lax.dot_general(wide, pair, (((1,), (1,)), ((), ())), preferred_element_type=jnp.float32)
            total = pulled if total is None else total + pulled
        out[row * side : (row + 1) * side, :] = total


def labels_of(sent, start, block, panels):
    tile = sent[pl.ds(start + block // 2 * LABEL_ROWS, LABEL_ROWS), :].astype(jnp.float32).astype(jnp.int32)
    return tile[block % 2 * panels : (block % 2 + 1) * panels]


def fates_of(pulled):
    height, cells = pulled.shape
    grouped = pulled.reshape(height // CELL_TYPES, CELL_TYPES, cells)
    scale = CELL_TYPES / jnp.sum(grouped, axis=1, keepdims=True)
    return (grouped * scale).reshape(height, cells).astype(jnp.bfloat16)


def load(own, rows_hbm, cols_hbm, growth_hbm, last_hbm, blocks_hbm, growth, known, blk, rows, cols, small_sems, sems):
    chunk = blk.shape[0] // CHUNKS
    small = [
        pltpu.make_async_copy(rows_hbm, rows, small_sems.at[0]),
        pltpu.make_async_copy(cols_hbm, cols, small_sems.at[1]),
        pltpu.make_async_copy(growth_hbm, growth, small_sems.at[2]),
        pltpu.make_async_copy(last_hbm, known, small_sems.at[3]),
    ]
    copies = [
        pltpu.make_async_copy(blocks_hbm.at[0, pl.ds(i * chunk, chunk)], blk.at[pl.ds(i * chunk, chunk)], sems.at[i])
        for i in range(CHUNKS)
    ]
    for copy in small + copies:
        copy.start()
    return small, copies


def sort_slots(own, rows, cols, count, table, first_row):
    slots = table.shape[1]
    for row in range(own):
        count[row] = row * (slots // own)
    for n in range(slots):
        row = rows[0, n] - first_row
        place = count[row]
        count[row] = place + 1
        table[0, place] = n
        table[1, place] = cols[0, n] - first_row + BAND_REACH


def first_kernel(own, rows_hbm, cols_hbm, growth_hbm, first_hbm, last_hbm, blocks_hbm,
                 left_ref, mid_ref, right_ref, keep_ref, part_ref, table_ref, growth, known, blk,
                 rows, cols, labels, src, acc, count, table, small_sems, sems):
    side = blk.shape[1]
    slots = blk.shape[0]
    first_row = lax.axis_index("cell") * own
    reach, inner = BAND_REACH * side, own * side

    @pl.when(lax.axis_index("tm") == 0)
    def _():
        labels_copy = pltpu.make_async_copy(first_hbm, labels, small_sems.at[5])
        labels_copy.start()
        small, copies = load(
            own, rows_hbm, cols_hbm, growth_hbm, last_hbm, blocks_hbm, growth, known, blk, rows, cols, small_sems, sems
        )
        small[0].wait()
        small[1].wait()
        sort_slots(own, rows, cols, count, table, first_row)
        table_copy = pltpu.make_async_copy(table, table_ref, small_sems.at[4])
        table_copy.start()
        small[2].wait()
        small[3].wait()
        labels_copy.wait()
        for b in range(own):
            cells = pl.ds(b * side, side)
            inverse = 1.0 / growth[0:1, cells]
            hot = one_hot(labels[:, cells])
            src[pl.ds(b * side, side), :] = jnp.where(hot, inverse, 0.0).astype(jnp.bfloat16)
        acc[...] = jnp.zeros_like(acc)
        for n in range(slots):
            if n % (slots // CHUNKS) == 0:
                copies[n // (slots // CHUNKS)].wait()
            row = rows_of(rows[0, n] - first_row, side)
            col = rows_of(cols[0, n] - first_row + BAND_REACH, side)
            acc[col, :] += jnp.dot(src[row, :], blk[n], preferred_element_type=jnp.float32)
        left_ref[0:reach, :] = acc[0:reach, :].astype(jnp.bfloat16)
        mid_ref[...] = acc[reach : reach + inner, :].astype(jnp.bfloat16)
        right_ref[0:reach, :] = acc[reach + inner :, :].astype(jnp.bfloat16)
        keep_ref[...] = acc[reach : reach + inner, :]
        for b in range(0, own, 2):
            pair = [known[:, pl.ds((b + i) * side, side)] for i in range(2)]
            tall = jnp.concatenate(pair, axis=0).astype(jnp.float32).astype(jnp.bfloat16)
            left_ref[pl.ds(reach + b * LABEL_ROWS // 2, LABEL_ROWS), :] = tall
            right_ref[pl.ds(reach + b * LABEL_ROWS // 2, LABEL_ROWS), :] = tall
        total = acc[0:side, :]
        for w in range(1, own + 2 * BAND_REACH):
            total += acc[w * side : (w + 1) * side, :]
        sums = jnp.sum(jnp.transpose(total), axis=0, keepdims=True)
        part_ref[0:8, :] = jnp.broadcast_to(sums, (8, side))
        part_ref[8:16, :] = jnp.zeros((8, side), jnp.float32)
        table_copy.wait()


def prepare_kernel(own, rows_hbm, cols_hbm, growth_hbm, last_hbm, blocks_hbm, table_in, growth_in, known_in, blk_in,
                   table_ref, growth, known, blk, half_ref, rows, cols, count, table, small_sems, sems):
    side = blk.shape[1]
    slots = blk.shape[0]
    first_row = lax.axis_index("cell") * own

    @pl.when(lax.axis_index("tm") != 0)
    def _():
        small, copies = load(
            own, rows_hbm, cols_hbm, growth_hbm, last_hbm, blocks_hbm, growth, known, blk, rows, cols, small_sems, sems
        )
        small[0].wait()
        small[1].wait()
        sort_slots(own, rows, cols, count, table, first_row)
        table_copy = pltpu.make_async_copy(table, table_ref, small_sems.at[4])
        table_copy.start()
        small[2].wait()
        small[3].wait()
        for copy in copies:
            copy.wait()
        largest = blk[0]
        for n in range(1, slots):
            largest = jnp.maximum(largest, blk[n])
        largest = largest.astype(jnp.float32)
        top = jnp.max(jnp.max(largest, axis=0, keepdims=True), axis=1, keepdims=True)
        power = jnp.round(jnp.log2(jnp.clip(top, 2.0**-126, 2.0**126)))
        half_ref[...] = jnp.broadcast_to(jnp.round(0.5 * power), half_ref.shape)
        table_copy.wait()


def second_kernel(own, table_ref, growth_ref, known_ref, left_ref, mid_ref, right_ref, part_in, half_ref, blk,
                  to_left, to_mid, to_right, keep_ref, part_ref, table, src, acc, fated, pulled, sem):
    side = blk.shape[1]
    slots = blk.shape[0]
    here = lax.axis_index("cell")
    reach, inner = BAND_REACH * side, own * side

    @pl.when(lax.axis_index("tm") == 0)
    def _():
        part_ref[...] = part_in[...]

    @pl.when(lax.axis_index("tm") != 0)
    def _():
        table_copy = pltpu.make_async_copy(table_ref, table, sem)
        table_copy.start()
        has_left, has_right = here > 0, here < lax.axis_size("cell") - 1
        mass = []
        for b in range(own):
            at = pl.ds(b * side, side)
            aside = jnp.where(has_left, left_ref[at, :].astype(jnp.float32), 0.0)
            aside += jnp.where(has_right, right_ref[at, :].astype(jnp.float32), 0.0)
            to_mid[pl.ds(inner + b * side, side), :] = aside.astype(jnp.bfloat16)
            mass.append(aside + mid_ref[at, :].astype(jnp.float32))
        top = functools.reduce(jnp.maximum, mass)
        top = jnp.max(top, axis=1, keepdims=True)
        power = jnp.round(jnp.log2(jnp.clip(top, 2.0**-126, 2.0**126)))
        half = half_ref[0:1, 0:1]
        for b in range(own):
            at = pl.ds(b * side, side)
            scaled = (mass[b] * jnp.exp2(-power) * jnp.exp2(-half)).astype(jnp.bfloat16)
            grown = scaled.astype(jnp.float32) / growth_ref[0:1, at]
            src[at, :] = grown.astype(jnp.bfloat16)
        acc[...] = jnp.zeros_like(acc)
        table_copy.wait()
        for n in range(slots):
            row = n // (slots // own) * side
            col = rows_of(table[1, n], side)
            acc[col, :] += jnp.dot(src[row : row + side, :], blk[table[0, n]], preferred_element_type=jnp.float32)
        power_row = as_row(power + half, side)
        to_left[pl.ds(inner, reach), :] = acc[0:reach, :].astype(jnp.bfloat16)
        to_right[pl.ds(inner, reach), :] = acc[reach + inner :, :].astype(jnp.bfloat16)
        keep_ref[...] = acc[reach : reach + inner, :]
        tall = jnp.concatenate([power_row, power_row], axis=0).astype(jnp.bfloat16)
        to_left[pl.ds(inner + reach, 16), :] = tall
        to_right[pl.ds(inner + reach, 16), :] = tall
        total = acc[0:side, :]
        for w in range(1, own + 2 * BAND_REACH):
            total += acc[w * side : (w + 1) * side, :]
        sums = jnp.sum(jnp.transpose(total), axis=0, keepdims=True)
        part_ref[0:8, :] = jnp.broadcast_to(sums, (8, side))
        part_ref[8:16, :] = power_row

        panels = known_ref.shape[0]
        for w in range(own + 2 * BAND_REACH):
            if w < BAND_REACH:
                labels = labels_of(left_ref, reach, w, panels)
            elif w < BAND_REACH + own:
                labels = known_ref[:, pl.ds((w - BAND_REACH) * side, side)]
            else:
                labels = labels_of(right_ref, reach, w - BAND_REACH - own, panels)
            fated[pl.ds(w * side, side), :] = jnp.where(one_hot(labels), 1.0, 0.0).astype(jnp.bfloat16)
        pull_backward(table, fated, blk, pulled, own)
        for b in range(own):
            at = pl.ds(b * side, side)
            fates = fates_of(pulled[at, :])
            to_left[at, :] = fates
            to_mid[at, :] = fates
            to_right[at, :] = fates


def combined(parts):
    top = functools.reduce(jnp.maximum, [part[8:16] for part in parts])
    total = sum(part[0:8] * jnp.exp2(part[8:16] - top) for part in parts)
    return total, top


def combine_kernel(count, *refs):
    mine, back_left, back_right, out, to_swap = refs[count:]
    inner = mine.shape[0] // 2
    rest = back_left.shape[0] - inner

    @pl.when(lax.axis_index("tm") == 0)
    def _():
        to_swap[0:rest, :] = back_left[inner:, :]
        to_swap[rest : 2 * rest, :] = back_right[inner:, :]

    @pl.when(lax.axis_index("tm") != 0)
    def _():
        to_swap[0 : 2 * inner, :] = mine[...]

    total, top = combined([part[...] for part in refs[:count]])
    out[0:8, :] = total
    out[8:16, :] = top


def last_kernel(own, all_cells, table_ref, whole, own_part, keep_first, keep_second, back_left, back_right, swap,
                mine_ref, blk, mass_ref, fate_ref, table, fated, pulled, sem):
    side = blk.shape[1]
    reach, inner = BAND_REACH * side, own * side
    here = lax.axis_index("cell")
    total, top = whole[0:8, :], whole[8:16, :]

    @pl.when(lax.axis_index("tm") == 0)
    def _():
        table_copy = pltpu.make_async_copy(table_ref, table, sem)
        table_copy.start()
        fated[0:reach, :] = back_left[0:reach, :]
        fated[reach : reach + inner, :] = swap[0:inner, :]
        fated[reach + inner :, :] = back_right[0:reach, :]
        scale = all_cells / as_column(total[0:1], side)
        for b in range(own):
            at = pl.ds(b * side, side)
            mass = keep_first[at, :] + swap[pl.ds(inner + b * side, side), :].astype(jnp.float32)
            mass_ref[0, :, at] = (mass * scale).astype(jnp.bfloat16)
        table_copy.wait()
        pull_backward(table, fated, blk, pulled, own)
        for b in range(own):
            at = pl.ds(b * side, side)
            fate_ref[0, :, at] = fates_of(pulled[at, :])

    @pl.when(lax.axis_index("tm") != 0)
    def _():
        has_left, has_right = here > 0, here < lax.axis_size("cell") - 1
        scale = all_cells / as_column(total[0:1], side)
        own_scale = as_column(jnp.exp2(own_part[8:9] - top[0:1]), side)
        left_scale = as_column(jnp.exp2(swap[pl.ds(reach, 16), :][0:1].astype(jnp.float32) - top[0:1]), side)
        right_scale = as_column(jnp.exp2(swap[pl.ds(2 * reach + 16, 16), :][0:1].astype(jnp.float32) - top[0:1]), side)
        for b in range(own):
            at = pl.ds(b * side, side)
            on_right = pl.ds(reach + 16 + b * side, side)
            mass = keep_second[at, :] * own_scale
            mass += jnp.where(has_left, swap[at, :].astype(jnp.float32) * left_scale, 0.0)
            mass += jnp.where(has_right, swap[on_right, :].astype(jnp.float32) * right_scale, 0.0)
            mass_ref[0, :, at] = (mass * scale).astype(jnp.bfloat16)
            fate_ref[0, :, at] = mine_ref[at, :]


def across(array, distance, sender, both=False):
    count = lax.axis_size("cell")
    at = lambda core, c: core * count + c
    other = 1 - sender
    route = [(at(sender, c), at(other, c + distance)) for c in range(count) if 0 <= c + distance < count]
    if both:
        route += [(there, here) for here, there in route]
    return lax.ppermute(array, ("tm", "cell"), route)


def flipped(array, bits):
    return lax.ppermute(array, "cell", [(c, c ^ bits) for c in range(lax.axis_size("cell"))])


def on_device(block_rows, block_cols, block_values, growth, first_labels, last_labels):
    cell_count = lax.axis_size("cell")
    side = block_values.shape[2]
    slots = block_values.shape[1]
    cells = growth.shape[1]
    own = cells // side
    panels = first_labels.shape[0]
    height = panels * CELL_TYPES
    window = own + 2 * BAND_REACH
    reach, inner = BAND_REACH * side, own * side

    vmem = pl.BlockSpec(memory_space=pltpu.VMEM)
    hbm = pl.BlockSpec(memory_space=pltpu.HBM)
    anywhere = pl.BlockSpec(memory_space=pl.ANY)
    bf16 = lambda *shape: jax.ShapeDtypeStruct(shape, jnp.bfloat16)
    f32 = lambda *shape: jax.ShapeDtypeStruct(shape, jnp.float32)
    i32 = lambda *shape: jax.ShapeDtypeStruct(shape, jnp.int32)
    params = pltpu.CompilerParams(vmem_limit_bytes=16 * 1024 * 1024)
    sem = pltpu.SemaphoreType.DMA
    slot_scratch = [pltpu.SMEM((1, slots), jnp.int32), pltpu.SMEM((1, slots), jnp.int32)]
    sort_scratch = [pltpu.SMEM((own,), jnp.int32), pltpu.SMEM((2, slots), jnp.int32)]
    loaded = (i32(2, slots), f32(1, cells), i32(panels, cells), bf16(slots, side, side))
    inputs = [pltpu.with_memory_space_constraint(array, pltpu.HBM) for array in (
        block_rows, block_cols, growth, first_labels, last_labels, block_values
    )]

    left, mid, right, keep_first, part, *loads = pl.pallas_call(
        functools.partial(first_kernel, own),
        out_shape=(
            bf16(reach + own * LABEL_ROWS // 2, side), bf16(inner, side), bf16(reach + own * LABEL_ROWS // 2, side), f32(inner, side),
            f32(16, side), *loaded,
        ),
        in_specs=[hbm] * 6,
        out_specs=[vmem] * 9,
        scratch_shapes=slot_scratch + [
            pltpu.VMEM((panels, cells), jnp.int32), pltpu.VMEM((inner, side), jnp.bfloat16),
            pltpu.VMEM((window * side, side), jnp.float32),
        ] + sort_scratch + [sem((6,)), sem((CHUNKS,))],
        compiler_params=params,
        name="push_first",
    )(*inputs)

    from_left = across(right, 1, 0)
    from_right = across(left, -1, 0)
    from_mid = across(mid, 0, 0, both=True)

    table, rates, known, blocks, half = pl.pallas_call(
        functools.partial(prepare_kernel, own),
        out_shape=loaded + (f32(8, side),),
        in_specs=[hbm] * 5 + [vmem] * 4,
        out_specs=[vmem] * 5,
        scratch_shapes=slot_scratch + sort_scratch + [sem((6,)), sem((CHUNKS,))],
        input_output_aliases={5 + i: i for i in range(4)},
        compiler_params=params,
        name="prepare",
    )(*inputs[:3], *inputs[4:], *loads)

    to_left, to_mid, to_right, keep_second, part = pl.pallas_call(
        functools.partial(second_kernel, own),
        out_shape=(
            bf16(inner + reach + 16, side), bf16(2 * inner, side), bf16(inner + reach + 16, side),
            f32(inner, side), f32(16, side),
        ),
        in_specs=[vmem] * 9,
        out_specs=[vmem] * 5,
        scratch_shapes=[
            pltpu.SMEM((2, slots), jnp.int32), pltpu.VMEM((inner, side), jnp.bfloat16), pltpu.VMEM((window * side, side), jnp.float32),
            pltpu.VMEM((window * side, side), jnp.bfloat16), pltpu.VMEM((inner, side), jnp.float32), sem,
        ],
        compiler_params=params,
        name="push_second_pull_first",
    )(table, rates, known, from_left, from_mid, from_right, part, half, blocks)

    back_left = across(to_right, 1, 1)
    back_right = across(to_left, -1, 1)

    whole = part
    bit = 1
    while bit < cell_count:
        if bit > 1:
            whole = jnp.concatenate(combined(parts), axis=0)
        parts = [whole] + [flipped(whole, k * bit) for k in range(1, 4) if k * bit < cell_count]
        bit *= 4
    whole, to_swap = pl.pallas_call(
        functools.partial(combine_kernel, len(parts)),
        out_shape=(f32(16, side), bf16(2 * max(inner, reach + 16), side)),
        in_specs=[vmem] * (len(parts) + 3),
        out_specs=[vmem] * 2,
        compiler_params=params,
        name="combine",
    )(*parts, to_mid, back_left, back_right)

    swap = across(to_swap, 0, 0, both=True)

    forward_mass, fate = pl.pallas_call(
        functools.partial(last_kernel, own, float(cells * cell_count)),
        out_shape=(bf16(1, height, cells), bf16(1, height, cells)),
        in_specs=[vmem] * 10,
        out_specs=[vmem] * 2,
        scratch_shapes=[
            pltpu.SMEM((2, slots), jnp.int32), pltpu.VMEM((window * side, side), jnp.bfloat16),
            pltpu.VMEM((inner, side), jnp.float32), sem,
        ],
        compiler_params=params,
        name="pull_second_normalise",
    )(table, whole, part, keep_first, keep_second, back_left, back_right, swap, to_mid, blocks)
    return forward_mass, fate


def solution(mesh):
    placed = (
        P("tm", "cell"),
        P("tm", "cell"),
        P("tm", "cell", None, None),
        P("tm", "cell"),
        P(None, "cell"),
        P(None, "cell"),
    )
    return jax.shard_map(
        on_device,
        mesh=mesh,
        in_specs=placed,
        out_specs=(P("tm", None, "cell"), P("tm", None, "cell")),
        check_vma=False,
    )
```

```python
import functools
import jax
import jax.numpy as jnp
from jax import lax
from jax.experimental import pallas as pl
from jax.experimental.pallas import tpu as pltpu
from jax.sharding import PartitionSpec as P

CELL_TYPES = 16
BAND_REACH = 4
LABEL_ROWS = 16
CHUNKS = 2


def rows_of(block, side):
    return pl.ds(pl.multiple_of(block * side, side), side)


def as_column(row, side):
    return jnp.transpose(jnp.broadcast_to(row, (side, side)))


def as_row(column, side):
    return jnp.transpose(jnp.broadcast_to(column, (side, side)))[0:8]


def one_hot(labels):
    types = lax.broadcasted_iota(jnp.int32, (CELL_TYPES, labels.shape[1]), 0)
    return jnp.concatenate([labels[p : p + 1] == types for p in range(labels.shape[0])], axis=0)


def pull_backward(table, src, blk, out, own):
    side = blk.shape[-1]
    per_row = blk.shape[0] // own
    for row in range(own):
        total = None
        for first in range(row * per_row, (row + 1) * per_row, 2):
            slots = [table[0, first], table[0, first + 1]]
            spots = [rows_of(table[1, first], side), rows_of(table[1, first + 1], side)]
            wide = jnp.concatenate([src[spot, :] for spot in spots], axis=1)
            pair = jnp.concatenate([blk[slot] for slot in slots], axis=1)
            pulled = lax.dot_general(wide, pair, (((1,), (1,)), ((), ())), preferred_element_type=jnp.float32)
            total = pulled if total is None else total + pulled
        out[row * side : (row + 1) * side, :] = total


def labels_of(sent, start, block, panels):
    tile = sent[pl.ds(start + block // 2 * LABEL_ROWS, LABEL_ROWS), :].astype(jnp.float32).astype(jnp.int32)
    return tile[block % 2 * panels : (block % 2 + 1) * panels]


def fates_of(pulled):
    height, cells = pulled.shape
    grouped = pulled.reshape(height // CELL_TYPES, CELL_TYPES, cells)
    scale = CELL_TYPES / jnp.sum(grouped, axis=1, keepdims=True)
    return (grouped * scale).reshape(height, cells).astype(jnp.bfloat16)


def load(own, rows_hbm, cols_hbm, growth_hbm, last_hbm, blocks_hbm, growth, known, blk, rows, cols, small_sems, sems):
    chunk = blk.shape[0] // CHUNKS
    small = [
        pltpu.make_async_copy(rows_hbm, rows, small_sems.at[0]),
        pltpu.make_async_copy(cols_hbm, cols, small_sems.at[1]),
        pltpu.make_async_copy(growth_hbm, growth, small_sems.at[2]),
        pltpu.make_async_copy(last_hbm, known, small_sems.at[3]),
    ]
    copies = [
        pltpu.make_async_copy(blocks_hbm.at[0, pl.ds(i * chunk, chunk)], blk.at[pl.ds(i * chunk, chunk)], sems.at[i])
        for i in range(CHUNKS)
    ]
    for copy in small + copies:
        copy.start()
    return small, copies


def sort_slots(own, rows, cols, count, table, first_row):
    slots = table.shape[1]
    for row in range(own):
        count[row] = row * (slots // own)
    for n in range(slots):
        row = rows[0, n] - first_row
        place = count[row]
        count[row] = place + 1
        table[0, place] = n
        table[1, place] = cols[0, n] - first_row + BAND_REACH


def first_kernel(own, rows_hbm, cols_hbm, growth_hbm, first_hbm, last_hbm, blocks_hbm,
                 left_ref, mid_ref, right_ref, keep_ref, part_ref, table_ref, growth, known, blk,
                 rows, cols, labels, src, acc, count, table, small_sems, sems):
    side = blk.shape[1]
    slots = blk.shape[0]
    first_row = lax.axis_index("cell") * own
    reach, inner = BAND_REACH * side, own * side

    @pl.when(lax.axis_index("tm") == 0)
    def _():
        labels_copy = pltpu.make_async_copy(first_hbm, labels, small_sems.at[5])
        labels_copy.start()
        small, copies = load(
            own, rows_hbm, cols_hbm, growth_hbm, last_hbm, blocks_hbm, growth, known, blk, rows, cols, small_sems, sems
        )
        small[0].wait()
        small[1].wait()
        sort_slots(own, rows, cols, count, table, first_row)
        table_copy = pltpu.make_async_copy(table, table_ref, small_sems.at[4])
        table_copy.start()
        small[2].wait()
        small[3].wait()
        labels_copy.wait()
        for b in range(own):
            cells = pl.ds(b * side, side)
            inverse = 1.0 / growth[0:1, cells]
            hot = one_hot(labels[:, cells])
            src[pl.ds(b * side, side), :] = jnp.where(hot, inverse, 0.0).astype(jnp.bfloat16)
        acc[...] = jnp.zeros_like(acc)
        for n in range(slots):
            if n % (slots // CHUNKS) == 0:
                copies[n // (slots // CHUNKS)].wait()
            row = rows_of(rows[0, n] - first_row, side)
            col = rows_of(cols[0, n] - first_row + BAND_REACH, side)
            acc[col, :] += jnp.dot(src[row, :], blk[n], preferred_element_type=jnp.float32)
        left_ref[0:reach, :] = acc[0:reach, :].astype(jnp.bfloat16)
        mid_ref[...] = acc[reach : reach + inner, :].astype(jnp.bfloat16)
        right_ref[0:reach, :] = acc[reach + inner :, :].astype(jnp.bfloat16)
        keep_ref[...] = acc[reach : reach + inner, :]
        for b in range(0, own, 2):
            pair = [known[:, pl.ds((b + i) * side, side)] for i in range(2)]
            tall = jnp.concatenate(pair, axis=0).astype(jnp.float32).astype(jnp.bfloat16)
            left_ref[pl.ds(reach + b * LABEL_ROWS // 2, LABEL_ROWS), :] = tall
            right_ref[pl.ds(reach + b * LABEL_ROWS // 2, LABEL_ROWS), :] = tall
        total = acc[0:side, :]
        for w in range(1, own + 2 * BAND_REACH):
            total += acc[w * side : (w + 1) * side, :]
        sums = jnp.sum(jnp.transpose(total), axis=0, keepdims=True)
        part_ref[0:8, :] = jnp.broadcast_to(sums, (8, side))
        part_ref[8:16, :] = jnp.zeros((8, side), jnp.float32)
        table_copy.wait()


def prepare_kernel(own, rows_hbm, cols_hbm, growth_hbm, last_hbm, blocks_hbm, table_in, growth_in, known_in, blk_in,
                   table_ref, growth, known, blk, half_ref, rows, cols, count, table, small_sems, sems):
    side = blk.shape[1]
    slots = blk.shape[0]
    first_row = lax.axis_index("cell") * own

    @pl.when(lax.axis_index("tm") != 0)
    def _():
        small, copies = load(
            own, rows_hbm, cols_hbm, growth_hbm, last_hbm, blocks_hbm, growth, known, blk, rows, cols, small_sems, sems
        )
        small[0].wait()
        small[1].wait()
        sort_slots(own, rows, cols, count, table, first_row)
        table_copy = pltpu.make_async_copy(table, table_ref, small_sems.at[4])
        table_copy.start()
        small[2].wait()
        small[3].wait()
        for copy in copies:
            copy.wait()
        largest = blk[0]
        for n in range(1, slots):
            largest = jnp.maximum(largest, blk[n])
        largest = largest.astype(jnp.float32)
        top = jnp.max(jnp.max(largest, axis=0, keepdims=True), axis=1, keepdims=True)
        power = jnp.round(jnp.log2(jnp.clip(top, 2.0**-126, 2.0**126)))
        half_ref[...] = jnp.broadcast_to(jnp.round(0.5 * power), half_ref.shape)
        table_copy.wait()


def second_kernel(own, table_ref, growth_ref, known_ref, left_ref, mid_ref, right_ref, part_in, half_ref, blk,
                  to_left, to_mid, to_right, keep_ref, part_ref, table, src, acc, fated, pulled, sem):
    side = blk.shape[1]
    slots = blk.shape[0]
    here = lax.axis_index("cell")
    reach, inner = BAND_REACH * side, own * side

    @pl.when(lax.axis_index("tm") == 0)
    def _():
        part_ref[...] = part_in[...]

    @pl.when(lax.axis_index("tm") != 0)
    def _():
        table_copy = pltpu.make_async_copy(table_ref, table, sem)
        table_copy.start()
        panels = known_ref.shape[0]
        for w in range(own + 2 * BAND_REACH):
            if w < BAND_REACH:
                labels = labels_of(left_ref, reach, w, panels)
            elif w < BAND_REACH + own:
                labels = known_ref[:, pl.ds((w - BAND_REACH) * side, side)]
            else:
                labels = labels_of(right_ref, reach, w - BAND_REACH - own, panels)
            fated[pl.ds(w * side, side), :] = jnp.where(one_hot(labels), 1.0, 0.0).astype(jnp.bfloat16)
        table_copy.wait()
        pull_backward(table, fated, blk, pulled, own)
        has_left, has_right = here > 0, here < lax.axis_size("cell") - 1
        mass = []
        for b in range(own):
            at = pl.ds(b * side, side)
            aside = jnp.where(has_left, left_ref[at, :].astype(jnp.float32), 0.0)
            aside += jnp.where(has_right, right_ref[at, :].astype(jnp.float32), 0.0)
            to_mid[pl.ds(inner + b * side, side), :] = aside.astype(jnp.bfloat16)
            mass.append(aside + mid_ref[at, :].astype(jnp.float32))
        top = functools.reduce(jnp.maximum, mass)
        top = jnp.max(top, axis=1, keepdims=True)
        power = jnp.round(jnp.log2(jnp.clip(top, 2.0**-126, 2.0**126)))
        half = half_ref[0:1, 0:1]
        for b in range(own):
            at = pl.ds(b * side, side)
            scaled = (mass[b] * jnp.exp2(-power) * jnp.exp2(-half)).astype(jnp.bfloat16)
            grown = scaled.astype(jnp.float32) / growth_ref[0:1, at]
            src[at, :] = grown.astype(jnp.bfloat16)
        acc[...] = jnp.zeros_like(acc)
        for n in range(slots):
            row = n // (slots // own) * side
            col = rows_of(table[1, n], side)
            acc[col, :] += jnp.dot(src[row : row + side, :], blk[table[0, n]], preferred_element_type=jnp.float32)
        for b in range(own):
            at = pl.ds(b * side, side)
            fates = fates_of(pulled[at, :])
            to_left[at, :] = fates
            to_mid[at, :] = fates
            to_right[at, :] = fates
        power_row = as_row(power + half, side)
        to_left[pl.ds(inner, reach), :] = acc[0:reach, :].astype(jnp.bfloat16)
        to_right[pl.ds(inner, reach), :] = acc[reach + inner :, :].astype(jnp.bfloat16)
        keep_ref[...] = acc[reach : reach + inner, :]
        tall = jnp.concatenate([power_row, power_row], axis=0).astype(jnp.bfloat16)
        to_left[pl.ds(inner + reach, 16), :] = tall
        to_right[pl.ds(inner + reach, 16), :] = tall
        total = acc[0:side, :]
        for w in range(1, own + 2 * BAND_REACH):
            total += acc[w * side : (w + 1) * side, :]
        sums = jnp.sum(jnp.transpose(total), axis=0, keepdims=True)
        part_ref[0:8, :] = jnp.broadcast_to(sums, (8, side))
        part_ref[8:16, :] = power_row


def combined(parts):
    top = functools.reduce(jnp.maximum, [part[8:16] for part in parts])
    total = sum(part[0:8] * jnp.exp2(part[8:16] - top) for part in parts)
    return total, top


def combine_kernel(count, *refs):
    mine, back_left, back_right, out, to_swap = refs[count:]
    inner = mine.shape[0] // 2
    rest = back_left.shape[0] - inner

    @pl.when(lax.axis_index("tm") == 0)
    def _():
        to_swap[0:rest, :] = back_left[inner:, :]
        to_swap[rest : 2 * rest, :] = back_right[inner:, :]

    @pl.when(lax.axis_index("tm") != 0)
    def _():
        to_swap[0 : 2 * inner, :] = mine[...]

    total, top = combined([part[...] for part in refs[:count]])
    out[0:8, :] = total
    out[8:16, :] = top


def last_kernel(own, all_cells, table_ref, whole, own_part, keep_first, keep_second, back_left, back_right, swap,
                mine_ref, blk, mass_ref, fate_ref, table, fated, pulled, sem):
    side = blk.shape[1]
    reach, inner = BAND_REACH * side, own * side
    here = lax.axis_index("cell")
    total, top = whole[0:8, :], whole[8:16, :]

    @pl.when(lax.axis_index("tm") == 0)
    def _():
        table_copy = pltpu.make_async_copy(table_ref, table, sem)
        table_copy.start()
        fated[0:reach, :] = back_left[0:reach, :]
        fated[reach : reach + inner, :] = swap[0:inner, :]
        fated[reach + inner :, :] = back_right[0:reach, :]
        scale = all_cells / as_column(total[0:1], side)
        for b in range(own):
            at = pl.ds(b * side, side)
            mass = keep_first[at, :] + swap[pl.ds(inner + b * side, side), :].astype(jnp.float32)
            mass_ref[0, :, at] = (mass * scale).astype(jnp.bfloat16)
        table_copy.wait()
        pull_backward(table, fated, blk, pulled, own)
        for b in range(own):
            at = pl.ds(b * side, side)
            fate_ref[0, :, at] = fates_of(pulled[at, :])

    @pl.when(lax.axis_index("tm") != 0)
    def _():
        has_left, has_right = here > 0, here < lax.axis_size("cell") - 1
        scale = all_cells / as_column(total[0:1], side)
        own_scale = as_column(jnp.exp2(own_part[8:9] - top[0:1]), side)
        left_scale = as_column(jnp.exp2(swap[pl.ds(reach, 16), :][0:1].astype(jnp.float32) - top[0:1]), side)
        right_scale = as_column(jnp.exp2(swap[pl.ds(2 * reach + 16, 16), :][0:1].astype(jnp.float32) - top[0:1]), side)
        for b in range(own):
            at = pl.ds(b * side, side)
            on_right = pl.ds(reach + 16 + b * side, side)
            mass = keep_second[at, :] * own_scale
            mass += jnp.where(has_left, swap[at, :].astype(jnp.float32) * left_scale, 0.0)
            mass += jnp.where(has_right, swap[on_right, :].astype(jnp.float32) * right_scale, 0.0)
            mass_ref[0, :, at] = (mass * scale).astype(jnp.bfloat16)
            fate_ref[0, :, at] = mine_ref[at, :]


def across(array, distance, sender, both=False):
    count = lax.axis_size("cell")
    at = lambda core, c: core * count + c
    other = 1 - sender
    route = [(at(sender, c), at(other, c + distance)) for c in range(count) if 0 <= c + distance < count]
    if both:
        route += [(there, here) for here, there in route]
    return lax.ppermute(array, ("tm", "cell"), route)


def flipped(array, bits):
    return lax.ppermute(array, "cell", [(c, c ^ bits) for c in range(lax.axis_size("cell"))])


def on_device(block_rows, block_cols, block_values, growth, first_labels, last_labels):
    cell_count = lax.axis_size("cell")
    side = block_values.shape[2]
    slots = block_values.shape[1]
    cells = growth.shape[1]
    own = cells // side
    panels = first_labels.shape[0]
    height = panels * CELL_TYPES
    window = own + 2 * BAND_REACH
    reach, inner = BAND_REACH * side, own * side

    vmem = pl.BlockSpec(memory_space=pltpu.VMEM)
    hbm = pl.BlockSpec(memory_space=pltpu.HBM)
    anywhere = pl.BlockSpec(memory_space=pl.ANY)
    bf16 = lambda *shape: jax.ShapeDtypeStruct(shape, jnp.bfloat16)
    f32 = lambda *shape: jax.ShapeDtypeStruct(shape, jnp.float32)
    i32 = lambda *shape: jax.ShapeDtypeStruct(shape, jnp.int32)
    params = pltpu.CompilerParams(vmem_limit_bytes=16 * 1024 * 1024)
    sem = pltpu.SemaphoreType.DMA
    slot_scratch = [pltpu.SMEM((1, slots), jnp.int32), pltpu.SMEM((1, slots), jnp.int32)]
    sort_scratch = [pltpu.SMEM((own,), jnp.int32), pltpu.SMEM((2, slots), jnp.int32)]
    loaded = (i32(2, slots), f32(1, cells), i32(panels, cells), bf16(slots, side, side))
    inputs = [pltpu.with_memory_space_constraint(array, pltpu.HBM) for array in (
        block_rows, block_cols, growth, first_labels, last_labels, block_values
    )]

    left, mid, right, keep_first, part, *loads = pl.pallas_call(
        functools.partial(first_kernel, own),
        out_shape=(
            bf16(reach + own * LABEL_ROWS // 2, side), bf16(inner, side), bf16(reach + own * LABEL_ROWS // 2, side), f32(inner, side),
            f32(16, side), *loaded,
        ),
        in_specs=[hbm] * 6,
        out_specs=[vmem] * 9,
        scratch_shapes=slot_scratch + [
            pltpu.VMEM((panels, cells), jnp.int32), pltpu.VMEM((inner, side), jnp.bfloat16),
            pltpu.VMEM((window * side, side), jnp.float32),
        ] + sort_scratch + [sem((6,)), sem((CHUNKS,))],
        compiler_params=params,
        name="push_first",
    )(*inputs)

    from_left = across(right, 1, 0)
    from_right = across(left, -1, 0)
    from_mid = across(mid, 0, 0, both=True)

    table, rates, known, blocks, half = pl.pallas_call(
        functools.partial(prepare_kernel, own),
        out_shape=loaded + (f32(8, side),),
        in_specs=[hbm] * 5 + [vmem] * 4,
        out_specs=[vmem] * 5,
        scratch_shapes=slot_scratch + sort_scratch + [sem((6,)), sem((CHUNKS,))],
        input_output_aliases={5 + i: i for i in range(4)},
        compiler_params=params,
        name="prepare",
    )(*inputs[:3], *inputs[4:], *loads)

    to_left, to_mid, to_right, keep_second, part = pl.pallas_call(
        functools.partial(second_kernel, own),
        out_shape=(
            bf16(inner + reach + 16, side), bf16(2 * inner, side), bf16(inner + reach + 16, side),
            f32(inner, side), f32(16, side),
        ),
        in_specs=[vmem] * 9,
        out_specs=[vmem] * 5,
        scratch_shapes=[
            pltpu.SMEM((2, slots), jnp.int32), pltpu.VMEM((inner, side), jnp.bfloat16), pltpu.VMEM((window * side, side), jnp.float32),
            pltpu.VMEM((window * side, side), jnp.bfloat16), pltpu.VMEM((inner, side), jnp.float32), sem,
        ],
        compiler_params=params,
        name="push_second_pull_first",
    )(table, rates, known, from_left, from_mid, from_right, part, half, blocks)

    back_left = across(to_right, 1, 1)
    back_right = across(to_left, -1, 1)

    whole = part
    bit = 1
    while bit < cell_count:
        if bit > 1:
            whole = jnp.concatenate(combined(parts), axis=0)
        parts = [whole] + [flipped(whole, k * bit) for k in range(1, 4) if k * bit < cell_count]
        bit *= 4
    whole, to_swap = pl.pallas_call(
        functools.partial(combine_kernel, len(parts)),
        out_shape=(f32(16, side), bf16(2 * max(inner, reach + 16), side)),
        in_specs=[vmem] * (len(parts) + 3),
        out_specs=[vmem] * 2,
        compiler_params=params,
        name="combine",
    )(*parts, to_mid, back_left, back_right)

    swap = across(to_swap, 0, 0, both=True)

    forward_mass, fate = pl.pallas_call(
        functools.partial(last_kernel, own, float(cells * cell_count)),
        out_shape=(bf16(1, height, cells), bf16(1, height, cells)),
        in_specs=[vmem] * 10,
        out_specs=[vmem] * 2,
        scratch_shapes=[
            pltpu.SMEM((2, slots), jnp.int32), pltpu.VMEM((window * side, side), jnp.bfloat16),
            pltpu.VMEM((inner, side), jnp.float32), sem,
        ],
        compiler_params=params,
        name="pull_second_normalise",
    )(table, whole, part, keep_first, keep_second, back_left, back_right, swap, to_mid, blocks)
    return forward_mass, fate


def solution(mesh):
    placed = (
        P("tm", "cell"),
        P("tm", "cell"),
        P("tm", "cell", None, None),
        P("tm", "cell"),
        P(None, "cell"),
        P(None, "cell"),
    )
    return jax.shard_map(
        on_device,
        mesh=mesh,
        in_specs=placed,
        out_specs=(P("tm", None, "cell"), P("tm", None, "cell")),
        check_vma=False,
    )
```

```python
import functools
import jax
import jax.numpy as jnp
from jax import lax
from jax.experimental import pallas as pl
from jax.experimental.pallas import tpu as pltpu
from jax.sharding import PartitionSpec as P

CELL_TYPES = 16
BAND_REACH = 4
LABEL_ROWS = 16
CHUNKS = 2
XA = ("inc", "chain", "full")
XB = ("inc", "inc", "full")
XC = "full"


def rows_of(block, side):
    return pl.ds(pl.multiple_of(block * side, side), side)


def as_column(row, side):
    return jnp.transpose(jnp.broadcast_to(row, (side, side)))


def as_row(column, side):
    return jnp.transpose(jnp.broadcast_to(column, (side, side)))[0:8]


def one_hot(labels):
    types = lax.broadcasted_iota(jnp.int32, (CELL_TYPES, labels.shape[1]), 0)
    return jnp.concatenate([labels[p : p + 1] == types for p in range(labels.shape[0])], axis=0)


def pull_backward(table, src, blk, out, own):
    side = blk.shape[-1]
    per_row = blk.shape[0] // own
    for row in range(own):
        total = None
        for first in range(row * per_row, (row + 1) * per_row, 2):
            slots = [table[0, first], table[0, first + 1]]
            spots = [rows_of(table[1, first], side), rows_of(table[1, first + 1], side)]
            wide = jnp.concatenate([src[spot, :] for spot in spots], axis=1)
            pair = jnp.concatenate([blk[slot] for slot in slots], axis=1)
            pulled = lax.dot_general(wide, pair, (((1,), (1,)), ((), ())), preferred_element_type=jnp.float32)
            total = pulled if total is None else total + pulled
        out[row * side : (row + 1) * side, :] = total


def labels_of(sent, start, block, panels):
    tile = sent[pl.ds(start + block // 2 * LABEL_ROWS, LABEL_ROWS), :].astype(jnp.float32).astype(jnp.int32)
    return tile[block % 2 * panels : (block % 2 + 1) * panels]


def fates_of(pulled):
    height, cells = pulled.shape
    grouped = pulled.reshape(height // CELL_TYPES, CELL_TYPES, cells)
    scale = CELL_TYPES / jnp.sum(grouped, axis=1, keepdims=True)
    return (grouped * scale).reshape(height, cells).astype(jnp.bfloat16)


def load(own, rows_hbm, cols_hbm, growth_hbm, last_hbm, blocks_hbm, growth, known, blk, rows, cols, small_sems, sems):
    chunk = blk.shape[0] // CHUNKS
    small = [
        pltpu.make_async_copy(rows_hbm, rows, small_sems.at[0]),
        pltpu.make_async_copy(cols_hbm, cols, small_sems.at[1]),
        pltpu.make_async_copy(growth_hbm, growth, small_sems.at[2]),
        pltpu.make_async_copy(last_hbm, known, small_sems.at[3]),
    ]
    copies = [
        pltpu.make_async_copy(blocks_hbm.at[0, pl.ds(i * chunk, chunk)], blk.at[pl.ds(i * chunk, chunk)], sems.at[i])
        for i in range(CHUNKS)
    ]
    for copy in small + copies:
        copy.start()
    return small, copies


def sort_slots(own, rows, cols, count, table, first_row):
    slots = table.shape[1]
    for row in range(own):
        count[row] = row * (slots // own)
    for n in range(slots):
        row = rows[0, n] - first_row
        place = count[row]
        count[row] = place + 1
        table[0, place] = n
        table[1, place] = cols[0, n] - first_row + BAND_REACH


def first_kernel(own, rows_hbm, cols_hbm, growth_hbm, first_hbm, last_hbm, blocks_hbm,
                 left_ref, mid_ref, right_ref, keep_ref, part_ref, table_ref, growth, known, blk,
                 rows, cols, labels, src, acc, count, table, small_sems, sems):
    side = blk.shape[1]
    slots = blk.shape[0]
    first_row = lax.axis_index("cell") * own
    reach, inner = BAND_REACH * side, own * side

    @pl.when(lax.axis_index("tm") == 0)
    def _():
        labels_copy = pltpu.make_async_copy(first_hbm, labels, small_sems.at[5])
        labels_copy.start()
        small, copies = load(
            own, rows_hbm, cols_hbm, growth_hbm, last_hbm, blocks_hbm, growth, known, blk, rows, cols, small_sems, sems
        )
        small[0].wait()
        small[1].wait()
        sort_slots(own, rows, cols, count, table, first_row)
        table_copy = pltpu.make_async_copy(table, table_ref, small_sems.at[4])
        table_copy.start()
        small[2].wait()
        small[3].wait()
        labels_copy.wait()
        for b in range(own):
            cells = pl.ds(b * side, side)
            inverse = 1.0 / growth[0:1, cells]
            hot = one_hot(labels[:, cells])
            src[pl.ds(b * side, side), :] = jnp.where(hot, inverse, 0.0).astype(jnp.bfloat16)
        acc[...] = jnp.zeros_like(acc)
        for n in range(slots):
            if n % (slots // CHUNKS) == 0:
                copies[n // (slots // CHUNKS)].wait()
            row = rows_of(rows[0, n] - first_row, side)
            col = rows_of(cols[0, n] - first_row + BAND_REACH, side)
            acc[col, :] += jnp.dot(src[row, :], blk[n], preferred_element_type=jnp.float32)
        left_ref[0:reach, :] = acc[0:reach, :].astype(jnp.bfloat16)
        mid_ref[...] = acc[reach : reach + inner, :].astype(jnp.bfloat16)
        right_ref[0:reach, :] = acc[reach + inner :, :].astype(jnp.bfloat16)
        keep_ref[...] = acc[reach : reach + inner, :]
        for b in range(0, own, 2):
            pair = [known[:, pl.ds((b + i) * side, side)] for i in range(2)]
            tall = jnp.concatenate(pair, axis=0).astype(jnp.float32).astype(jnp.bfloat16)
            left_ref[pl.ds(reach + b * LABEL_ROWS // 2, LABEL_ROWS), :] = tall
            right_ref[pl.ds(reach + b * LABEL_ROWS // 2, LABEL_ROWS), :] = tall
        total = acc[0:side, :]
        for w in range(1, own + 2 * BAND_REACH):
            total += acc[w * side : (w + 1) * side, :]
        sums = jnp.sum(jnp.transpose(total), axis=0, keepdims=True)
        part_ref[0:8, :] = jnp.broadcast_to(sums, (8, side))
        part_ref[8:16, :] = jnp.zeros((8, side), jnp.float32)
        table_copy.wait()


def prepare_kernel(own, rows_hbm, cols_hbm, growth_hbm, last_hbm, blocks_hbm, table_in, growth_in, known_in, blk_in,
                   table_ref, growth, known, blk, half_ref, rows, cols, count, table, small_sems, sems):
    side = blk.shape[1]
    slots = blk.shape[0]
    first_row = lax.axis_index("cell") * own

    @pl.when(lax.axis_index("tm") != 0)
    def _():
        small, copies = load(
            own, rows_hbm, cols_hbm, growth_hbm, last_hbm, blocks_hbm, growth, known, blk, rows, cols, small_sems, sems
        )
        small[0].wait()
        small[1].wait()
        sort_slots(own, rows, cols, count, table, first_row)
        table_copy = pltpu.make_async_copy(table, table_ref, small_sems.at[4])
        table_copy.start()
        small[2].wait()
        small[3].wait()
        for copy in copies:
            copy.wait()
        largest = blk[0]
        for n in range(1, slots):
            largest = jnp.maximum(largest, blk[n])
        largest = largest.astype(jnp.float32)
        top = jnp.max(jnp.max(largest, axis=0, keepdims=True), axis=1, keepdims=True)
        power = jnp.round(jnp.log2(jnp.clip(top, 2.0**-126, 2.0**126)))
        half_ref[...] = jnp.broadcast_to(jnp.round(0.5 * power), half_ref.shape)
        table_copy.wait()


def second_kernel(own, table_ref, growth_ref, known_ref, left_ref, mid_ref, right_ref, part_in, half_ref, blk,
                  to_left, to_mid, to_right, keep_ref, part_ref, table, src, acc, fated, pulled, sem):
    side = blk.shape[1]
    slots = blk.shape[0]
    here = lax.axis_index("cell")
    reach, inner = BAND_REACH * side, own * side

    @pl.when(lax.axis_index("tm") == 0)
    def _():
        part_ref[...] = part_in[...]

    @pl.when(lax.axis_index("tm") != 0)
    def _():
        table_copy = pltpu.make_async_copy(table_ref, table, sem)
        table_copy.start()
        has_left, has_right = here > 0, here < lax.axis_size("cell") - 1
        mass = []
        for b in range(own):
            at = pl.ds(b * side, side)
            aside = jnp.where(has_left, left_ref[at, :].astype(jnp.float32), 0.0)
            aside += jnp.where(has_right, right_ref[at, :].astype(jnp.float32), 0.0)
            to_mid[pl.ds(inner + b * side, side), :] = aside.astype(jnp.bfloat16)
            mass.append(aside + mid_ref[at, :].astype(jnp.float32))
        top = functools.reduce(jnp.maximum, mass)
        top = jnp.max(top, axis=1, keepdims=True)
        power = jnp.round(jnp.log2(jnp.clip(top, 2.0**-126, 2.0**126)))
        half = half_ref[0:1, 0:1]
        for b in range(own):
            at = pl.ds(b * side, side)
            scaled = (mass[b] * jnp.exp2(-power) * jnp.exp2(-half)).astype(jnp.bfloat16)
            grown = scaled.astype(jnp.float32) / growth_ref[0:1, at]
            src[at, :] = grown.astype(jnp.bfloat16)
        acc[...] = jnp.zeros_like(acc)
        table_copy.wait()
        for n in range(slots):
            row = n // (slots // own) * side
            col = rows_of(table[1, n], side)
            acc[col, :] += jnp.dot(src[row : row + side, :], blk[table[0, n]], preferred_element_type=jnp.float32)
        power_row = as_row(power + half, side)
        to_left[pl.ds(inner, reach), :] = acc[0:reach, :].astype(jnp.bfloat16)
        to_right[pl.ds(inner, reach), :] = acc[reach + inner :, :].astype(jnp.bfloat16)
        keep_ref[...] = acc[reach : reach + inner, :]
        tall = jnp.concatenate([power_row, power_row], axis=0).astype(jnp.bfloat16)
        to_left[pl.ds(inner + reach, 16), :] = tall
        to_right[pl.ds(inner + reach, 16), :] = tall
        total = acc[0:side, :]
        for w in range(1, own + 2 * BAND_REACH):
            total += acc[w * side : (w + 1) * side, :]
        sums = jnp.sum(jnp.transpose(total), axis=0, keepdims=True)
        part_ref[0:8, :] = jnp.broadcast_to(sums, (8, side))
        part_ref[8:16, :] = power_row

        panels = known_ref.shape[0]
        for w in range(own + 2 * BAND_REACH):
            if w < BAND_REACH:
                labels = labels_of(left_ref, reach, w, panels)
            elif w < BAND_REACH + own:
                labels = known_ref[:, pl.ds((w - BAND_REACH) * side, side)]
            else:
                labels = labels_of(right_ref, reach, w - BAND_REACH - own, panels)
            fated[pl.ds(w * side, side), :] = jnp.where(one_hot(labels), 1.0, 0.0).astype(jnp.bfloat16)
        pull_backward(table, fated, blk, pulled, own)
        for b in range(own):
            at = pl.ds(b * side, side)
            fates = fates_of(pulled[at, :])
            to_left[at, :] = fates
            to_mid[at, :] = fates
            to_right[at, :] = fates


def combined(parts):
    top = functools.reduce(jnp.maximum, [part[8:16] for part in parts])
    total = sum(part[0:8] * jnp.exp2(part[8:16] - top) for part in parts)
    return total, top


def combine_kernel(count, *refs):
    mine, back_left, back_right, out, to_swap = refs[count:]
    inner = mine.shape[0] // 2
    rest = back_left.shape[0] - inner

    @pl.when(lax.axis_index("tm") == 0)
    def _():
        to_swap[0:rest, :] = back_left[inner:, :]
        to_swap[rest : 2 * rest, :] = back_right[inner:, :]

    @pl.when(lax.axis_index("tm") != 0)
    def _():
        to_swap[0 : 2 * inner, :] = mine[...]

    total, top = combined([part[...] for part in refs[:count]])
    out[0:8, :] = total
    out[8:16, :] = top


def last_kernel(own, all_cells, table_ref, whole, own_part, keep_first, keep_second, back_left, back_right, swap,
                mine_ref, blk, mass_ref, fate_ref, table, fated, pulled, sem):
    side = blk.shape[1]
    reach, inner = BAND_REACH * side, own * side
    here = lax.axis_index("cell")
    total, top = whole[0:8, :], whole[8:16, :]

    @pl.when(lax.axis_index("tm") == 0)
    def _():
        table_copy = pltpu.make_async_copy(table_ref, table, sem)
        table_copy.start()
        fated[0:reach, :] = back_left[0:reach, :]
        fated[reach : reach + inner, :] = swap[0:inner, :]
        fated[reach + inner :, :] = back_right[0:reach, :]
        scale = all_cells / as_column(total[0:1], side)
        for b in range(own):
            at = pl.ds(b * side, side)
            mass = keep_first[at, :] + swap[pl.ds(inner + b * side, side), :].astype(jnp.float32)
            mass_ref[0, :, at] = (mass * scale).astype(jnp.bfloat16)
        table_copy.wait()
        pull_backward(table, fated, blk, pulled, own)
        for b in range(own):
            at = pl.ds(b * side, side)
            fate_ref[0, :, at] = fates_of(pulled[at, :])

    @pl.when(lax.axis_index("tm") != 0)
    def _():
        has_left, has_right = here > 0, here < lax.axis_size("cell") - 1
        scale = all_cells / as_column(total[0:1], side)
        own_scale = as_column(jnp.exp2(own_part[8:9] - top[0:1]), side)
        left_scale = as_column(jnp.exp2(swap[pl.ds(reach, 16), :][0:1].astype(jnp.float32) - top[0:1]), side)
        right_scale = as_column(jnp.exp2(swap[pl.ds(2 * reach + 16, 16), :][0:1].astype(jnp.float32) - top[0:1]), side)
        for b in range(own):
            at = pl.ds(b * side, side)
            on_right = pl.ds(reach + 16 + b * side, side)
            mass = keep_second[at, :] * own_scale
            mass += jnp.where(has_left, swap[at, :].astype(jnp.float32) * left_scale, 0.0)
            mass += jnp.where(has_right, swap[on_right, :].astype(jnp.float32) * right_scale, 0.0)
            mass_ref[0, :, at] = (mass * scale).astype(jnp.bfloat16)
            fate_ref[0, :, at] = mine_ref[at, :]


def across(array, distance, sender, mode):
    count = lax.axis_size("cell")
    at = lambda core, c: core * count + c
    other = 1 - sender
    route = {at(sender, c): at(other, c + distance) for c in range(count) if 0 <= c + distance < count}
    if mode == "full":
        for c in range(count):
            route[at(other, c)] = at(sender, c - distance) if 0 <= c - distance < count else at(other, c)
            route.setdefault(at(sender, c), at(sender, c))
    if mode == "chain":
        for c in range(count):
            route[at(other, c)] = at(sender, c)
            route.setdefault(at(sender, c), at(other, (c + distance) % count))
    return lax.ppermute(array, ("tm", "cell"), list(route.items()))


def flipped(array, bits):
    return lax.ppermute(array, "cell", [(c, c ^ bits) for c in range(lax.axis_size("cell"))])


def on_device(block_rows, block_cols, block_values, growth, first_labels, last_labels):
    cell_count = lax.axis_size("cell")
    side = block_values.shape[2]
    slots = block_values.shape[1]
    cells = growth.shape[1]
    own = cells // side
    panels = first_labels.shape[0]
    height = panels * CELL_TYPES
    window = own + 2 * BAND_REACH
    reach, inner = BAND_REACH * side, own * side

    vmem = pl.BlockSpec(memory_space=pltpu.VMEM)
    hbm = pl.BlockSpec(memory_space=pltpu.HBM)
    anywhere = pl.BlockSpec(memory_space=pl.ANY)
    bf16 = lambda *shape: jax.ShapeDtypeStruct(shape, jnp.bfloat16)
    f32 = lambda *shape: jax.ShapeDtypeStruct(shape, jnp.float32)
    i32 = lambda *shape: jax.ShapeDtypeStruct(shape, jnp.int32)
    params = pltpu.CompilerParams(vmem_limit_bytes=16 * 1024 * 1024)
    sem = pltpu.SemaphoreType.DMA
    slot_scratch = [pltpu.SMEM((1, slots), jnp.int32), pltpu.SMEM((1, slots), jnp.int32)]
    sort_scratch = [pltpu.SMEM((own,), jnp.int32), pltpu.SMEM((2, slots), jnp.int32)]
    loaded = (i32(2, slots), f32(1, cells), i32(panels, cells), bf16(slots, side, side))
    inputs = [pltpu.with_memory_space_constraint(array, pltpu.HBM) for array in (
        block_rows, block_cols, growth, first_labels, last_labels, block_values
    )]

    left, mid, right, keep_first, part, *loads = pl.pallas_call(
        functools.partial(first_kernel, own),
        out_shape=(
            bf16(reach + own * LABEL_ROWS // 2, side), bf16(inner, side), bf16(reach + own * LABEL_ROWS // 2, side), f32(inner, side),
            f32(16, side), *loaded,
        ),
        in_specs=[hbm] * 6,
        out_specs=[vmem] * 9,
        scratch_shapes=slot_scratch + [
            pltpu.VMEM((panels, cells), jnp.int32), pltpu.VMEM((inner, side), jnp.bfloat16),
            pltpu.VMEM((window * side, side), jnp.float32),
        ] + sort_scratch + [sem((6,)), sem((CHUNKS,))],
        compiler_params=params,
        name="push_first",
    )(*inputs)

    from_left = across(right, 1, 0, XA[0])
    from_right = across(left, -1, 0, XA[1])
    from_mid = across(mid, 0, 0, XA[2])

    table, rates, known, blocks, half = pl.pallas_call(
        functools.partial(prepare_kernel, own),
        out_shape=loaded + (f32(8, side),),
        in_specs=[hbm] * 5 + [vmem] * 4,
        out_specs=[vmem] * 5,
        scratch_shapes=slot_scratch + sort_scratch + [sem((6,)), sem((CHUNKS,))],
        input_output_aliases={5 + i: i for i in range(4)},
        compiler_params=params,
        name="prepare",
    )(*inputs[:3], *inputs[4:], *loads)

    to_left, to_mid, to_right, keep_second, part = pl.pallas_call(
        functools.partial(second_kernel, own),
        out_shape=(
            bf16(inner + reach + 16, side), bf16(2 * inner, side), bf16(inner + reach + 16, side),
            f32(inner, side), f32(16, side),
        ),
        in_specs=[vmem] * 9,
        out_specs=[vmem] * 5,
        scratch_shapes=[
            pltpu.SMEM((2, slots), jnp.int32), pltpu.VMEM((inner, side), jnp.bfloat16), pltpu.VMEM((window * side, side), jnp.float32),
            pltpu.VMEM((window * side, side), jnp.bfloat16), pltpu.VMEM((inner, side), jnp.float32), sem,
        ],
        compiler_params=params,
        name="push_second_pull_first",
    )(table, rates, known, from_left, from_mid, from_right, part, half, blocks)

    back_left = across(to_right, 1, 1, XB[0])
    back_right = across(to_left, -1, 1, XB[1])

    whole = part
    bit = 1
    while bit < cell_count:
        if bit > 1:
            whole = jnp.concatenate(combined(parts), axis=0)
        parts = [whole] + [flipped(whole, k * bit) for k in range(1, 4) if k * bit < cell_count]
        bit *= 4
    whole, to_swap = pl.pallas_call(
        functools.partial(combine_kernel, len(parts)),
        out_shape=(f32(16, side), bf16(2 * max(inner, reach + 16), side)),
        in_specs=[vmem] * (len(parts) + 3),
        out_specs=[vmem] * 2,
        compiler_params=params,
        name="combine",
    )(*parts, to_mid, back_left, back_right)

    swap = across(to_swap, 0, 0, XC)

    forward_mass, fate = pl.pallas_call(
        functools.partial(last_kernel, own, float(cells * cell_count)),
        out_shape=(bf16(1, height, cells), bf16(1, height, cells)),
        in_specs=[vmem] * 10,
        out_specs=[vmem] * 2,
        scratch_shapes=[
            pltpu.SMEM((2, slots), jnp.int32), pltpu.VMEM((window * side, side), jnp.bfloat16),
            pltpu.VMEM((inner, side), jnp.float32), sem,
        ],
        compiler_params=params,
        name="pull_second_normalise",
    )(table, whole, part, keep_first, keep_second, back_left, back_right, swap, to_mid, blocks)
    return forward_mass, fate


def solution(mesh):
    placed = (
        P("tm", "cell"),
        P("tm", "cell"),
        P("tm", "cell", None, None),
        P("tm", "cell"),
        P(None, "cell"),
        P(None, "cell"),
    )
    return jax.shard_map(
        on_device,
        mesh=mesh,
        in_specs=placed,
        out_specs=(P("tm", None, "cell"), P("tm", None, "cell")),
        check_vma=False,
    )
```
